32 devices in a mesh: member: 2 (over y), gx: 4 (over z), gy: 4 (over x, core).
Axes of the slice: x: 2, y: 2, z: 4, core: 2. Of those that a mesh axis runs over, the one named last changes fastest.
Arguments:
- checkpoint: float32 [8, 4, 4, 12288], P(('member', 'gx'), 'gy'), parts along dimension 0, may hold values from -6 to 6
- holder_list: int32 [8, 4, 4], P(('member', 'gx'), 'gy'), parts along dimension 0, may hold values from 0 to 3, each once within a row
- height: float32 [64, 512], P(('member', 'gx'), 'gy'), parts along dimension 0, may hold values from -6 to 6
- land_mask: int32 [32, 512], P('gx', 'gy'), may hold values 0 or 1
- diffusivity: float32 [3, 16], replicated, may hold values from 0.02 to 0.2
- tracer_weight: float32 [6, 16, 32, 512], P('member', None, 'gx', 'gy'), parts along dimension 0, may hold values from -6 to 6
- height_weight: float32 [64, 512], P(('member', 'gx'), 'gy'), parts along dimension 0, may hold values from -6 to 6
Outputs:
- adjoint_tracers: float32 [6, 16, 32, 512], P('member', None, 'gx', 'gy'), parts along dimension 0
- adjoint_height: float32 [64, 512], P(('member', 'gx'), 'gy'), parts along dimension 0
The draws below stay inside these ranges and needn't reach their ends.
There are 2 independent parts, one for each index of `member`. The reference program is written for one: setup_inputs(seed, part) draws one part's arguments, and reference() takes and returns one part's arrays. A program takes and returns all parts, laid end to end along the dimension named above; an argument that names none is the same for every part. Nothing has to cross between parts.
Inputs may be any that keep to these rules, and one draw needn't show every extreme that they name: For each owner device (o, g), holder_list[o, g, :] names every longitude index once: each device along gx holds exactly one piece of every owner's tracers in its row.
All inputs are finite; a program needn't handle non-finite values. No bound on the sum of `land_mask` on one device may be relied on, other than what follows from the above.
Results may differ from the reference program's by a relative error of at most 0.0001.
Values sent between devices are 32-bit elements; how exact they have to be, the bound alone decides.
A program may use at most 64 MiB of HBM per device.

```python
import math
import jax
import jax.numpy as jnp
from jax import lax

CX = 8
CY = 128
LEV = 16
ITERS = 4
NX = 32
NY = 512
PIECE = 12288
N_GX = 4
N_GY = 4


def plant(drawn, key, low, top_value):
    extent = drawn.shape
    place = [jax.random.randint(jax.random.fold_in(key, axis), (), 0, extent[axis]) for axis in range(len(extent))]
    drawn = drawn.at[tuple(place)].set(low)
    longest = extent.index(max(extent))
    place[longest] = (place[longest] + 1) % extent[longest]
    return drawn.at[tuple(place)].set(top_value)


def steps_of(stream_key, dims, shards, least, high):
    loudness = 1.0
    for position, parts in shards:
        steps = jax.random.uniform(jax.random.fold_in(jax.random.fold_in(stream_key, 6), position), (parts,), jnp.float32, least / len(shards), high / len(shards))
        loudness = loudness * jnp.repeat(jnp.exp(steps), dims[position] // parts).reshape((-1,) + (1,) * (len(dims) - 1 - position))
    return loudness


def normal_values(rng, extent, deviation, reach, shards=(), dtype=jnp.bfloat16):
    drawn = deviation * jax.random.normal(rng, extent, jnp.float32)
    if shards:
        drawn = drawn * steps_of(rng, extent, shards, -0.22, 0.18)
    return jnp.clip(drawn, -reach, reach).astype(dtype)


def setup_inputs(seed: int = 0, part: int = 0) -> dict:
    key_of = jax.random.split(jax.random.key(seed), 8)
    part_splits = jax.random.split(jax.random.fold_in(key_of[7], part), 8)
    checkpoint = normal_values(part_splits[0], (N_GX, N_GY, N_GX, PIECE), 1.0, 6.0, ((0, 4), (1, 4)), jnp.float32)
    holder_list = jax.vmap(lambda own: jax.random.permutation(own, N_GX))(jax.random.split(part_splits[1], N_GX * N_GY)).reshape((N_GX, N_GY, N_GX)).astype(jnp.int32)
    height = normal_values(part_splits[2], (NX, NY), 1.0, 6.0, ((0, 4), (1, 4)), jnp.float32)
    land_mask = plant((jax.random.randint(key_of[3], (NX, NY), 0, 4) < 3).astype(jnp.int32), jax.random.fold_in(key_of[3], 1), 0, 1)
    diffusivity = jnp.clip(jnp.exp(jax.random.uniform(key_of[4], (3, LEV), jnp.float32, math.log(0.02), math.log(0.2))), 0.02, 0.2)
    tracer_weight = normal_values(part_splits[5], (3, LEV, NX, NY), 1.0, 6.0, ((2, 4), (3, 4)), jnp.float32)
    height_weight = normal_values(part_splits[6], (NX, NY), 1.0, 6.0, ((0, 4), (1, 4)), jnp.float32)
    return dict(checkpoint=checkpoint, holder_list=holder_list, height=height, land_mask=land_mask, diffusivity=diffusivity, tracer_weight=tracer_weight, height_weight=height_weight)


ADVECTION = 0.3
VERTICAL_MIX = 0.1
HEIGHT_DIFFUSION = 0.2
HEIGHT_DAMPING = 0.3
BUOYANCY = 0.5

def pad_field(field):
    field = jnp.concatenate([field[..., -1:, :], field, field[..., :1, :]], axis=-2)
    widths = [(0, 0)] * (field.ndim - 1) + [(1, 1)]
    return jnp.pad(field, widths)

def advance(height_pad, tracer_pad, wet_cells, diffusivity):
    east_cell = tracer_pad[..., 2:, 1:-1]
    west_cell = tracer_pad[..., :-2, 1:-1]
    north_cell = tracer_pad[..., 1:-1, 2:]
    south_cell = tracer_pad[..., 1:-1, :-2]
    centre = tracer_pad[..., 1:-1, 1:-1]
    height_mid = height_pad[1:-1, 1:-1]
    zonal = -0.5 * (height_pad[1:-1, 2:] - height_pad[1:-1, :-2])
    meridional = 0.5 * (height_pad[2:, 1:-1] - height_pad[:-2, 1:-1])
    advect = zonal * 0.5 * (east_cell - west_cell) + meridional * 0.5 * (north_cell - south_cell)
    laplace = east_cell + west_cell + north_cell + south_cell - 4.0 * centre
    upper = jnp.concatenate([centre[:, :1], centre[:, :-1]], axis=1)
    lower = jnp.concatenate([centre[:, 1:], centre[:, -1:]], axis=1)
    vertical = upper + lower - 2.0 * centre
    tracer_new = centre + wet_cells * (-ADVECTION * advect + diffusivity[:, :, None, None] * laplace + VERTICAL_MIX * vertical)
    height_lap = height_pad[2:, 1:-1] + height_pad[:-2, 1:-1] + height_pad[1:-1, 2:] + height_pad[1:-1, :-2] - 4.0 * height_mid
    height_new = height_mid + HEIGHT_DIFFUSION * height_lap - HEIGHT_DAMPING * jnp.tanh(height_mid) + BUOYANCY * wet_cells * lax.optimization_barrier(jnp.mean(centre[0], axis=0))
    return (height_new, tracer_new)

def reference(checkpoint, holder_list, height, land_mask, diffusivity, tracer_weight, height_weight):
    by_owner = jnp.transpose(checkpoint, (2, 1, 0, 3))
    pieces = jnp.take_along_axis(by_owner, holder_list[..., None].astype(jnp.int32), axis=2)
    pieces = pieces.reshape(N_GX, N_GY, 3, LEV, CX, CY)
    tracers = jnp.transpose(pieces, (2, 3, 0, 4, 1, 5)).reshape(3, LEV, NX, NY)
    wet_cells = land_mask.astype(jnp.float32)

    def forward(tracer_start, height_start):
        tracer_now, height_now = (tracer_start, height_start)
        for repeat in range(ITERS):
            height_now, tracer_now = advance(pad_field(height_now), pad_field(tracer_now), wet_cells, diffusivity)
        return (tracer_now, height_now)
    outputs, pullback = jax.vjp(forward, tracers, height)
    adjoint_tracers, adjoint_height = pullback((tracer_weight, height_weight))
    return (adjoint_tracers, adjoint_height)
```

```python
import functools
import jax
import jax.numpy as jnp
from jax import lax
from jax.experimental import pallas as pl
from jax.experimental.pallas import tpu as pltpu
from jax.sharding import PartitionSpec as P

ITERS = 4
ADVECTION = 0.3
VERTICAL_MIX = 0.1
HEIGHT_DIFFUSION = 0.2
HEIGHT_DAMPING = 0.3
BUOYANCY = 0.5

SUB = 8
LANE = 128
MESH = pl.DeviceIdType.MESH


def roll_lanes(value, shift):
    return pltpu.roll(value, shift, 1)


def roll_rows(value, shift):
    return pltpu.roll(value, shift, 0)


def kernel(
    n, n_y, levels, piece_rows,
    holder_ref, diff_ref, ckpt_ref, height_ref, mask_ref, tw_hbm, hw_ref,
    out_ref, outh_ref,
    buf, recv, state, dy, tw, lam, mu, wet, arow, brow, mrow, gurow, gvrow,
    packs, packr, slab_s, slab_r, bpacks, bpackr,
    a2a_send, a2a_recv, f_send, f_recv, b_send, b_recv, tw_sem,
):
    me = lax.axis_index("gx")
    my = lax.axis_index("gy")
    east, west = lax.rem(me + 1, n), lax.rem(me + n - 1, n)
    north, south = lax.rem(my + 1, n_y), lax.rem(my + n_y - 1, n_y)
    channels = 3 * levels
    tiles = channels // SUB
    per = levels // SUB
    hrow = channels
    padded = -(-piece_rows // SUB) * SUB

    tw_copy = pltpu.make_async_copy(tw_hbm, tw, tw_sem)
    tw_copy.start()

    barrier = pltpu.get_barrier_semaphore()
    for k in range(1, n):
        pl.semaphore_signal(barrier, inc=1, device_id={"gx": lax.rem(me + k, n)}, device_id_type=MESH)
    for other in (north, south):
        pl.semaphore_signal(barrier, inc=1, device_id={"gy": other}, device_id_type=MESH)

    depth = 0 if piece_rows % SUB else piece_rows // SUB
    if padded != piece_rows:
        buf[...] = jnp.zeros_like(buf)
    for o in range(0, n, SUB):
        size = min(SUB, n - o)
        for r in range(piece_rows):
            row = r % SUB * depth + r // SUB if depth else r
            buf[pl.ds(o * padded + row, size, stride=padded), :] = ckpt_ref[o:o + size, r * LANE:(r + 1) * LANE]

    pl.semaphore_wait(barrier, n + 1)

    mine = pl.multiple_of(me * padded, SUB)
    sends = []
    a2a = []
    for k in range(1, n):
        owner = lax.rem(me + k, n)
        copy = pltpu.make_async_remote_copy(
            src_ref=buf.at[pl.ds(pl.multiple_of(owner * padded, SUB), padded)],
            dst_ref=recv.at[me],
            send_sem=a2a_send.at[k], recv_sem=a2a_recv.at[k],
            device_id={"gx": owner}, device_id_type=MESH,
        )
        copy.start()
        a2a.append(copy)
    recv[me] = buf[pl.ds(mine, padded), :]

    lane = lax.broadcasted_iota(jnp.int32, (SUB, LANE), 1)
    sub = lax.broadcasted_iota(jnp.int32, (SUB, LANE), 0)
    first_lane, last_lane = lane == 0, lane == LANE - 1
    edge_lane = first_lane | last_lane
    first_row, last_row = sub == 0, sub == SUB - 1
    pair = lax.shift_right_logical(lane, 1)
    even = (lane & 1) == 0
    zero = jnp.zeros((SUB, LANE), jnp.float32)

    diff = []
    for t in range(tiles):
        value = zero
        for s in range(SUB):
            channel = t * SUB + s
            value = jnp.where(sub == s, diff_ref[channel // levels, channel % levels], value)
        diff.append(value)
    wet_tile = mask_ref[...].astype(jnp.float32)
    wet[...] = wet_tile
    for t in range(tiles):
        rows = pl.ds(t * SUB, SUB)
        mu[0, rows, :] = zero
        mu[SUB + 1, rows, :] = zero
    for t in range(ITERS):
        arow[t, 0:SUB, :] = zero
        arow[t, SUB:2 * SUB, :] = zero
    tw_copy.wait()
    for x in range(SUB):
        for t in range(tiles):
            lam[x, t * SUB:(t + 1) * SUB, :] = tw[pl.ds(t * SUB * SUB + x, SUB, stride=SUB), :]

    for copy in a2a:
        copy.wait_recv()
    for p in range(n):
        holder = holder_ref[0, 0, p]
        if depth:
            for x in range(SUB):
                state[0, x + 1, p * depth:(p + 1) * depth, :] = recv[holder, x * depth:(x + 1) * depth, :]
        else:
            for r in range(piece_rows):
                row = p * piece_rows + r
                state[0, row % SUB + 1, row // SUB:row // SUB + 1, :] = recv[holder, r:r + 1, :]

    def exchange(send_east, recv_east, send_west, recv_west, pack_out, pack_in, send_sem, recv_sem, step):
        route = (
            (send_east, recv_east, {"gx": east}),
            (send_west, recv_west, {"gx": west}),
            (pack_out, pack_in.at[step, 0], {"gy": north}),
            (pack_out, pack_in.at[step, 1], {"gy": south}),
        )
        copies = []
        for i, (source, target, device) in enumerate(route):
            copy = pltpu.make_async_remote_copy(
                src_ref=source, dst_ref=target, send_sem=send_sem.at[step, i], recv_sem=recv_sem.at[step, i],
                device_id=device, device_id_type=MESH,
            )
            copy.start()
            copies.append(copy)
        sends.extend(copies)
        return copies

    def unpacked(pack_in, step):
        from_south = jnp.where(my > 0, roll_lanes(pack_in[step, 0], 1), zero)
        from_north = jnp.where(my < n_y - 1, roll_lanes(pack_in[step, 1], LANE - 1), zero)
        return jnp.where(even, from_north, from_south)

    def spread(columns, k):
        return roll_lanes(columns, lax.rem(2 * LANE - 1 - 2 * k, LANE))

    def packed_with(packed, value, k):
        return jnp.where(pair == k, roll_lanes(value, 2 * k + 1), packed)

    def vertical(values):
        result = [None] * tiles
        for tracer in range(3):
            group = values[tracer * per:(tracer + 1) * per]
            down = [roll_rows(v, 1) for v in group]
            up = [roll_rows(v, SUB - 1) for v in group]
            for i, v in enumerate(group):
                upper = jnp.where(first_row, down[i - 1] if i else v, down[i])
                lower = jnp.where(last_row, up[i + 1] if i < per - 1 else v, up[i])
                result[tracer * per + i] = upper + lower - 2.0 * v
        return result

    def row_of(ref, x):
        return jnp.broadcast_to(ref[pl.ds(x, 1), :], (SUB, LANE))

    def send_state(step, packed, h):
        packs[step] = packed_with(packed, h, channels)
        state[step, 1, hrow:hrow + SUB, :] = jnp.broadcast_to(h[0:1, :], (SUB, LANE))
        state[step, SUB, hrow:hrow + SUB, :] = jnp.broadcast_to(h[SUB - 1:SUB, :], (SUB, LANE))
        return exchange(
            state.at[step, SUB], state.at[step, 0], state.at[step, 1], state.at[step, SUB + 1],
            packs.at[step], packr, f_send, f_recv, step,
        )

    hslot = channels

    def pack_body(x, packed):
        for t in range(tiles):
            packed = packed_with(packed, state[0, x + 1, t * SUB:(t + 1) * SUB, :], x * tiles + t)
        return packed

    heights = [height_ref[...]]
    copies = send_state(0, lax.fori_loop(0, SUB, pack_body, zero), heights[0])

    for step in range(ITERS):
        h = heights[step]
        final = step == ITERS - 1
        damp = jnp.tanh(h)
        for copy in copies:
            copy.wait_recv()
        columns = unpacked(packr, step)
        side = spread(columns, hslot)
        h_w = jnp.where(first_row, jnp.broadcast_to(state[step, 0, hrow:hrow + 1, :], (SUB, LANE)), roll_rows(h, 1))
        h_e = jnp.where(last_row, jnp.broadcast_to(state[step, SUB + 1, hrow:hrow + 1, :], (SUB, LANE)), roll_rows(h, SUB - 1))
        h_s = jnp.where(first_lane, side, roll_lanes(h, 1))
        h_n = jnp.where(last_lane, side, roll_lanes(h, LANE - 1))
        arow[step, 1:SUB + 1, :] = (-0.25 * ADVECTION) * (h_n - h_s)
        brow[step] = (0.25 * ADVECTION) * (h_e - h_w)

        def forward_body(x, packed):
            a = row_of(arow.at[step], x + 1)
            b = row_of(brow.at[step], x)
            w = row_of(wet, x)
            centre = [state[step, x + 1, t * SUB:(t + 1) * SUB, :] for t in range(tiles)]
            if not final:
                vert = vertical(centre)
                total = centre[0]
                for i in range(1, per):
                    total = total + centre[i]
                mrow[pl.ds(x, 1), :] = jnp.sum(total, axis=0, keepdims=True)
            for t in range(tiles):
                rows = slice(t * SUB, (t + 1) * SUB)
                c = centre[t]
                side = spread(columns, x * tiles + t)
                c_s = jnp.where(first_lane, side, roll_lanes(c, 1))
                c_n = jnp.where(last_lane, side, roll_lanes(c, LANE - 1))
                delta = c_n - c_s
                dy[step, x, rows, :] = delta
                if not final:
                    c_e = state[step, x + 2, rows, :]
                    c_w = state[step, x, rows, :]
                    lap = c_e + c_w + c_n + c_s - 4.0 * c
                    new = c + w * (diff[t] * lap - a * (c_e - c_w) - b * delta + VERTICAL_MIX * vert[t])
                    state[step + 1, x + 1, rows, :] = new
                    packed = packed_with(packed, new, x * tiles + t)
            return packed

        packed = lax.fori_loop(0, SUB, forward_body, zero)
        if not final:
            lap = h_e + h_w + h_n + h_s - 4.0 * h
            h = h + HEIGHT_DIFFUSION * lap - HEIGHT_DAMPING * damp + (BUOYANCY / levels) * wet_tile * mrow[...]
            heights.append(h)
            copies = send_state(step + 1, packed, h)

    lam_h = hw_ref[...]
    columns = None
    for step in reversed(range(ITERS)):

        def gather_body(x, packed):
            b = row_of(brow.at[step], x)
            w = row_of(wet, x)
            gu = zero
            gv = zero
            for t in range(tiles):
                rows = slice(t * SUB, (t + 1) * SUB)
                value = lam[x, rows, :]
                if columns is not None:
                    value = value + jnp.where(edge_lane, spread(columns, x * tiles + t), 0.0)
                    lam[x, rows, :] = value
                m = w * value
                mu[x + 1, rows, :] = m
                bm = b * m
                dm = diff[t] * m
                packed = packed_with(packed, jnp.where(last_lane, dm - bm, dm + bm), x * tiles + t)
                gu = gu + m * (state[step, x + 2, rows, :] - state[step, x, rows, :])
                gv = gv + m * dy[step, x, rows, :]
            gurow[pl.ds(x, 1), :] = jnp.sum(gu, axis=0, keepdims=True)
            gvrow[pl.ds(x, 1), :] = jnp.sum(gv, axis=0, keepdims=True)
            return packed

        packed = lax.fori_loop(0, SUB, gather_body, zero)
        gu = (-0.25 * ADVECTION) * gurow[...]
        gv = (-0.25 * ADVECTION) * gvrow[...]
        spread_h = HEIGHT_DIFFUSION * lam_h
        to_e, to_w, to_n, to_s = spread_h + gv, spread_h - gv, spread_h - gu, spread_h + gu
        bpacks[step] = packed_with(packed, jnp.where(last_lane, to_n, to_s), hslot)
        a_last = row_of(arow.at[step], SUB)
        a_first = row_of(arow.at[step], 1)
        for t in range(tiles):
            rows = slice(t * SUB, (t + 1) * SUB)
            slab_s[step, 0, rows, :] = (diff[t] - a_last) * mu[SUB, rows, :]
            slab_s[step, 1, rows, :] = (diff[t] + a_first) * mu[1, rows, :]
        slab_s[step, 0, hrow:hrow + SUB, :] = jnp.broadcast_to(to_e[SUB - 1:SUB, :], (SUB, LANE))
        slab_s[step, 1, hrow:hrow + SUB, :] = jnp.broadcast_to(to_w[0:1, :], (SUB, LANE))
        copies = exchange(
            slab_s.at[step, 0], slab_r.at[step, 0], slab_s.at[step, 1], slab_r.at[step, 1],
            bpacks.at[step], bpackr, b_send, b_recv, step,
        )

        source = (BUOYANCY / levels) * wet_tile * lam_h
        mrow[...] = source

        def local_body(x, carry):
            a_w = row_of(arow.at[step], x)
            a_e = row_of(arow.at[step], x + 2)
            b = row_of(brow.at[step], x)
            centre = [mu[x + 1, t * SUB:(t + 1) * SUB, :] for t in range(tiles)]
            vert = vertical(centre)
            push = row_of(mrow, x)
            for t in range(tiles):
                rows = slice(t * SUB, (t + 1) * SUB)
                m = centre[t]
                m_w = mu[x, rows, :]
                m_e = mu[x + 2, rows, :]
                bm = b * m
                dm = diff[t] * m
                from_s = jnp.where(first_lane, 0.0, roll_lanes(dm - bm, 1))
                from_n = jnp.where(last_lane, 0.0, roll_lanes(dm + bm, LANE - 1))
                value = lam[x, rows, :] + VERTICAL_MIX * vert[t] - 4.0 * dm + from_s + from_n
                value = value + diff[t] * (m_w + m_e) + (a_e * m_e - a_w * m_w)
                if t < per:
                    value = value + push
                lam[x, rows, :] = value
            return carry

        lax.fori_loop(0, SUB, local_body, 0)
        damp = jnp.tanh(heights[step])
        lam_h = (
            lam_h - 4.0 * spread_h - HEIGHT_DAMPING * (1.0 - damp * damp) * lam_h
            + jnp.where(first_row, 0.0, roll_rows(to_e, 1)) + jnp.where(last_row, 0.0, roll_rows(to_w, SUB - 1))
            + jnp.where(first_lane, 0.0, roll_lanes(to_n, 1)) + jnp.where(last_lane, 0.0, roll_lanes(to_s, LANE - 1))
        )
        for copy in copies:
            copy.wait_recv()
        columns = unpacked(bpackr, step)
        for t in range(tiles):
            rows = slice(t * SUB, (t + 1) * SUB)
            lam[0, rows, :] = lam[0, rows, :] + slab_r[step, 0, rows, :]
            lam[SUB - 1, rows, :] = lam[SUB - 1, rows, :] + slab_r[step, 1, rows, :]
        lam_h = lam_h + jnp.where(edge_lane, spread(columns, hslot), 0.0)
        lam_h = lam_h + jnp.where(first_row, jnp.broadcast_to(slab_r[step, 0, hrow:hrow + 1, :], (SUB, LANE)), 0.0)
        lam_h = lam_h + jnp.where(last_row, jnp.broadcast_to(slab_r[step, 1, hrow:hrow + 1, :], (SUB, LANE)), 0.0)

    outh_ref[...] = lam_h
    for x in range(SUB):
        for t in range(tiles):
            value = lam[x, t * SUB:(t + 1) * SUB, :] + jnp.where(edge_lane, spread(columns, x * tiles + t), 0.0)
            out_ref[pl.ds(t * SUB * SUB + x, SUB, stride=SUB), :] = value

    for copy in a2a + sends:
        copy.wait_send()


def local(checkpoint, holder_list, height, land_mask, diffusivity, tracer_weight, height_weight):
    n, n_y = lax.axis_size("gx"), lax.axis_size("gy")
    width_x, width_y = height.shape
    assert (width_x, width_y) == (SUB, LANE)
    levels = diffusivity.shape[1]
    channels = 3 * levels
    piece_rows = checkpoint.shape[3] // LANE
    padded = -(-piece_rows // SUB) * SUB
    rows = channels + SUB
    f32 = jnp.float32
    vmem = pl.BlockSpec(memory_space=pltpu.VMEM)
    smem = pl.BlockSpec(memory_space=pltpu.SMEM)
    tile = pltpu.VMEM((SUB, LANE), f32)
    out, out_h = pl.pallas_call(
        functools.partial(kernel, n, n_y, levels, piece_rows),
        out_shape=(
            jax.ShapeDtypeStruct((channels * SUB, LANE), f32),
            jax.ShapeDtypeStruct((SUB, LANE), f32),
        ),
        in_specs=[smem, smem, vmem, vmem, vmem, pl.BlockSpec(memory_space=pl.ANY), vmem],
        out_specs=(vmem, vmem),
        scratch_shapes=[
            pltpu.VMEM((n * padded, LANE), f32),
            pltpu.VMEM((n, padded, LANE), f32),
            pltpu.VMEM((ITERS, SUB + 2, rows, LANE), f32),
            pltpu.VMEM((ITERS, SUB, channels, LANE), f32),
            pltpu.VMEM((channels * SUB, LANE), f32),
            pltpu.VMEM((SUB, channels, LANE), f32),
            pltpu.VMEM((SUB + 2, channels, LANE), f32),
            tile,
            pltpu.VMEM((ITERS, 2 * SUB, LANE), f32),
            pltpu.VMEM((ITERS, SUB, LANE), f32),
            tile, tile, tile,
            pltpu.VMEM((ITERS, SUB, LANE), f32),
            pltpu.VMEM((ITERS, 2, SUB, LANE), f32),
            pltpu.VMEM((ITERS, 2, rows, LANE), f32),
            pltpu.VMEM((ITERS, 2, rows, LANE), f32),
            pltpu.VMEM((ITERS, SUB, LANE), f32),
            pltpu.VMEM((ITERS, 2, SUB, LANE), f32),
            pltpu.SemaphoreType.DMA((n,)),
            pltpu.SemaphoreType.DMA((n,)),
            pltpu.SemaphoreType.DMA((ITERS, 4)),
            pltpu.SemaphoreType.DMA((ITERS, 4)),
            pltpu.SemaphoreType.DMA((ITERS, 4)),
            pltpu.SemaphoreType.DMA((ITERS, 4)),
            pltpu.SemaphoreType.DMA,
        ],
        compiler_params=pltpu.CompilerParams(
            collective_id=0, has_side_effects=True, vmem_limit_bytes=32 * 2**20
        ),
    )(
        holder_list, diffusivity, checkpoint.reshape(checkpoint.shape[2:]), height, land_mask,
        tracer_weight.reshape(channels * SUB, LANE), height_weight,
    )
    return out.reshape(tracer_weight.shape), out_h


def solution(mesh):
    return jax.shard_map(
        local,
        mesh=mesh,
        in_specs=(
            P(("member", "gx"), "gy", None, None),
            P(("member", "gx"), "gy", None),
            P(("member", "gx"), "gy"),
            P("gx", "gy"),
            P(),
            P("member", None, "gx", "gy"),
            P(("member", "gx"), "gy"),
        ),
        out_specs=(P("member", None, "gx", "gy"), P(("member", "gx"), "gy")),
        check_vma=False,
    )
```

```python
import functools
import jax
import jax.numpy as jnp
from jax import lax
from jax.experimental import pallas as pl
from jax.experimental.pallas import tpu as pltpu
from jax.sharding import PartitionSpec as P

ITERS = 4
ADVECTION = 0.3
VERTICAL_MIX = 0.1
HEIGHT_DIFFUSION = 0.2
HEIGHT_DAMPING = 0.3
BUOYANCY = 0.5

SUB = 8
LANE = 128
MESH = pl.DeviceIdType.MESH


def roll_lanes(value, shift):
    return pltpu.roll(value, shift, 1)


def roll_rows(value, shift):
    return pltpu.roll(value, shift, 0)


def kernel(
    n, n_y, levels, piece_rows,
    holder_hbm, diff_hbm, ckpt_hbm, height_hbm, mask_hbm, tw_hbm, hw_hbm,
    out_ref, outh_ref,
    buf, recv, state, dy, tw, lam, mu, wet, arow, brow, mrow, gurow, gvrow,
    packs, packr, slab_s, slab_r, bpacks, bpackr,
    holder_ref, diff_ref, ckpt_ref, height_ref, mask_ref, hw_ref,
    a2a_send, a2a_recv, f_send, f_recv, b_send, b_recv, in_sem,
):
    me = lax.axis_index("gx")
    my = lax.axis_index("gy")
    east, west = lax.rem(me + 1, n), lax.rem(me + n - 1, n)
    north, south = lax.rem(my + 1, n_y), lax.rem(my + n_y - 1, n_y)
    channels = 3 * levels
    tiles = channels // SUB
    per = levels // SUB
    hrow = channels
    padded = -(-piece_rows // SUB) * SUB

    inputs = (
        (ckpt_hbm, ckpt_ref), (diff_hbm, diff_ref), (mask_hbm, mask_ref), (tw_hbm, tw),
        (height_hbm, height_ref), (hw_hbm, hw_ref), (holder_hbm, holder_ref),
    )
    loads = [pltpu.make_async_copy(source, target, in_sem.at[i]) for i, (source, target) in enumerate(inputs)]
    for load in loads:
        load.start()

    barrier = pltpu.get_barrier_semaphore()
    for k in range(1, n):
        pl.semaphore_signal(barrier, inc=1, device_id={"gx": lax.rem(me + k, n)}, device_id_type=MESH)
    for other in (north, south):
        pl.semaphore_signal(barrier, inc=1, device_id={"gy": other}, device_id_type=MESH)

    loads[0].wait()
    depth = 0 if piece_rows % SUB else piece_rows // SUB
    if padded != piece_rows:
        buf[...] = jnp.zeros_like(buf)
    for o in range(0, n, SUB):
        size = min(SUB, n - o)
        for r in range(piece_rows):
            row = r % SUB * depth + r // SUB if depth else r
            buf[pl.ds(o * padded + row, size, stride=padded), :] = ckpt_ref[o:o + size, r * LANE:(r + 1) * LANE]

    pl.semaphore_wait(barrier, n + 1)

    mine = pl.multiple_of(me * padded, SUB)
    sends = []
    a2a = []
    for k in range(1, n):
        owner = lax.rem(me + k, n)
        copy = pltpu.make_async_remote_copy(
            src_ref=buf.at[pl.ds(pl.multiple_of(owner * padded, SUB), padded)],
            dst_ref=recv.at[me],
            send_sem=a2a_send.at[k], recv_sem=a2a_recv.at[k],
            device_id={"gx": owner}, device_id_type=MESH,
        )
        copy.start()
        a2a.append(copy)
    recv[me] = buf[pl.ds(mine, padded), :]

    lane = lax.broadcasted_iota(jnp.int32, (SUB, LANE), 1)
    sub = lax.broadcasted_iota(jnp.int32, (SUB, LANE), 0)
    first_lane, last_lane = lane == 0, lane == LANE - 1
    edge_lane = first_lane | last_lane
    first_row, last_row = sub == 0, sub == SUB - 1
    pair = lax.shift_right_logical(lane, 1)
    even = (lane & 1) == 0
    zero = jnp.zeros((SUB, LANE), jnp.float32)

    for load in loads[1:]:
        load.wait()
    mrow[...] = zero
    diff = []
    for t in range(tiles):
        value = zero
        for s in range(SUB):
            channel = t * SUB + s
            value = jnp.where(sub == s, diff_ref[channel // levels, channel % levels], value)
        diff.append(value)
    wet_tile = mask_ref[...].astype(jnp.float32)
    wet[...] = wet_tile
    for t in range(tiles):
        rows = pl.ds(t * SUB, SUB)
        mu[0, rows, :] = zero
        mu[SUB + 1, rows, :] = zero
    for t in range(ITERS):
        arow[t, 0:SUB, :] = zero
        arow[t, SUB:2 * SUB, :] = zero
    for x in range(SUB):
        for t in range(tiles):
            lam[x, t * SUB:(t + 1) * SUB, :] = tw[pl.ds(t * SUB * SUB + x, SUB, stride=SUB), :]

    for copy in a2a:
        copy.wait_recv()
    for p in range(n):
        holder = holder_ref[0, 0, p]
        if depth:
            for x in range(SUB):
                state[0, x + 1, p * depth:(p + 1) * depth, :] = recv[holder, x * depth:(x + 1) * depth, :]
        else:
            for r in range(piece_rows):
                row = p * piece_rows + r
                state[0, row % SUB + 1, row // SUB:row // SUB + 1, :] = recv[holder, r:r + 1, :]

    def exchange(route, send_sem, recv_sem, step, first):
        copies = []
        for i, (source, target, device) in enumerate(route, first):
            copy = pltpu.make_async_remote_copy(
                src_ref=source, dst_ref=target, send_sem=send_sem.at[step, i], recv_sem=recv_sem.at[step, i],
                device_id=device, device_id_type=MESH,
            )
            copy.start()
            copies.append(copy)
        sends.extend(copies)
        return copies

    def exchange_rows(send_east, recv_east, send_west, recv_west, send_sem, recv_sem, step):
        route = ((send_east, recv_east, {"gx": east}), (send_west, recv_west, {"gx": west}))
        return exchange(route, send_sem, recv_sem, step, 0)

    def exchange_columns(pack_out, pack_in, send_sem, recv_sem, step):
        route = ((pack_out, pack_in.at[step, 0], {"gy": north}), (pack_out, pack_in.at[step, 1], {"gy": south}))
        return exchange(route, send_sem, recv_sem, step, 2)

    def wait_all(copies):
        for copy in copies:
            copy.wait_recv()

    def rows_of(body, first, last, carry):
        return lax.fori_loop(first, last, body, carry, unroll=3 if (last - first) % 3 == 0 else 4)

    def unpacked(pack_in, step):
        from_south = jnp.where(my > 0, roll_lanes(pack_in[step, 0], 1), zero)
        from_north = jnp.where(my < n_y - 1, roll_lanes(pack_in[step, 1], LANE - 1), zero)
        return jnp.where(even, from_north, from_south)

    def spread(columns, k):
        return roll_lanes(columns, lax.rem(2 * LANE - 1 - 2 * k, LANE))

    def packed_with(packed, value, k):
        return jnp.where(pair == k, roll_lanes(value, 2 * k + 1), packed)

    def vertical(values):
        result = [None] * tiles
        for tracer in range(3):
            group = values[tracer * per:(tracer + 1) * per]
            down = [roll_rows(v, 1) for v in group]
            up = [roll_rows(v, SUB - 1) for v in group]
            for i, v in enumerate(group):
                upper = jnp.where(first_row, down[i - 1] if i else v, down[i])
                lower = jnp.where(last_row, up[i + 1] if i < per - 1 else v, up[i])
                result[tracer * per + i] = upper + lower - 2.0 * v
        return result

    def row_of(ref, x):
        return jnp.broadcast_to(ref[pl.ds(x, 1), :], (SUB, LANE))

    hslot = channels

    def send_state(step, packed, h):
        state[step, 1, hrow:hrow + SUB, :] = jnp.broadcast_to(h[0:1, :], (SUB, LANE))
        state[step, SUB, hrow:hrow + SUB, :] = jnp.broadcast_to(h[SUB - 1:SUB, :], (SUB, LANE))
        row_copies = exchange_rows(
            state.at[step, SUB], state.at[step, 0], state.at[step, 1], state.at[step, SUB + 1], f_send, f_recv, step,
        )
        packs[step] = packed_with(packed, h, hslot)
        return row_copies, exchange_columns(packs.at[step], packr, f_send, f_recv, step)

    def pack_body(x, packed):
        for t in range(tiles):
            packed = packed_with(packed, state[0, x + 1, t * SUB:(t + 1) * SUB, :], x * tiles + t)
        return packed

    heights = [height_ref[...]]
    row_copies, column_copies = send_state(0, rows_of(pack_body, 0, SUB, zero), heights[0])

    for step in range(ITERS):
        h = heights[step]
        final = step == ITERS - 1
        damp = jnp.tanh(h)
        wait_all(column_copies)
        columns = unpacked(packr, step)
        side = spread(columns, hslot)
        h_s = jnp.where(first_lane, side, roll_lanes(h, 1))
        h_n = jnp.where(last_lane, side, roll_lanes(h, LANE - 1))
        h_w, h_e = roll_rows(h, 1), roll_rows(h, SUB - 1)
        arow[step, 1:SUB + 1, :] = (-0.25 * ADVECTION) * (h_n - h_s)
        brow[step] = (0.25 * ADVECTION) * (h_e - h_w)

        def forward_body(x, packed):
            a = row_of(arow.at[step], x + 1)
            b = row_of(brow.at[step], x)
            w = row_of(wet, x)
            centre = [state[step, x + 1, t * SUB:(t + 1) * SUB, :] for t in range(tiles)]
            if not final:
                vert = vertical(centre)
                total = centre[0]
                for i in range(1, per):
                    total = total + centre[i]
                mrow[pl.ds(x, 1), :] = jnp.sum(total, axis=0, keepdims=True)
            for t in range(tiles):
                rows = slice(t * SUB, (t + 1) * SUB)
                c = centre[t]
                side = spread(columns, x * tiles + t)
                c_s = jnp.where(first_lane, side, roll_lanes(c, 1))
                c_n = jnp.where(last_lane, side, roll_lanes(c, LANE - 1))
                delta = c_n - c_s
                dy[step, x, rows, :] = delta
                if not final:
                    c_e = state[step, x + 2, rows, :]
                    c_w = state[step, x, rows, :]
                    lap = c_e + c_w + c_n + c_s - 4.0 * c
                    new = c + w * (diff[t] * lap - a * (c_e - c_w) - b * delta + VERTICAL_MIX * vert[t])
                    state[step + 1, x + 1, rows, :] = new
                    packed = packed_with(packed, new, x * tiles + t)
            return packed

        if final:
            rows_of(forward_body, 0, SUB, zero)
            break
        packed = rows_of(forward_body, 1, SUB - 1, zero)
        wait_all(row_copies)
        h_w = jnp.where(first_row, jnp.broadcast_to(state[step, 0, hrow:hrow + 1, :], (SUB, LANE)), h_w)
        h_e = jnp.where(last_row, jnp.broadcast_to(state[step, SUB + 1, hrow:hrow + 1, :], (SUB, LANE)), h_e)
        brow[step] = (0.25 * ADVECTION) * (h_e - h_w)
        packed = forward_body(SUB - 1, forward_body(0, packed))
        lap = h_e + h_w + h_n + h_s - 4.0 * h
        h = h + HEIGHT_DIFFUSION * lap - HEIGHT_DAMPING * damp + (BUOYANCY / levels) * wet_tile * mrow[...]
        heights.append(h)
        row_copies, column_copies = send_state(step + 1, packed, h)

    def add_rows(step):
        for t in range(tiles):
            rows = slice(t * SUB, (t + 1) * SUB)
            lam[0, rows, :] = lam[0, rows, :] + slab_r[step, 0, rows, :]
            lam[SUB - 1, rows, :] = lam[SUB - 1, rows, :] + slab_r[step, 1, rows, :]

    def height_arrivals(step, lam_h, columns):
        lam_h = lam_h + jnp.where(edge_lane, spread(columns, hslot), 0.0)
        lam_h = lam_h + jnp.where(first_row, jnp.broadcast_to(slab_r[step, 0, hrow:hrow + 1, :], (SUB, LANE)), 0.0)
        return lam_h + jnp.where(last_row, jnp.broadcast_to(slab_r[step, 1, hrow:hrow + 1, :], (SUB, LANE)), 0.0)

    lam_h = hw_ref[...]
    columns = None
    for step in reversed(range(ITERS)):
        if step < ITERS - 1:
            wait_all(column_copies)
            columns = unpacked(bpackr, step + 1)

        def gather_body(x, packed):
            b = row_of(brow.at[step], x)
            w = row_of(wet, x)
            gu = zero
            gv = zero
            for t in range(tiles):
                rows = slice(t * SUB, (t + 1) * SUB)
                value = lam[x, rows, :]
                if columns is not None:
                    value = value + jnp.where(edge_lane, spread(columns, x * tiles + t), 0.0)
                    lam[x, rows, :] = value
                m = w * value
                mu[x + 1, rows, :] = m
                bm = b * m
                dm = diff[t] * m
                packed = packed_with(packed, jnp.where(last_lane, dm - bm, dm + bm), x * tiles + t)
                gu = gu + m * (state[step, x + 2, rows, :] - state[step, x, rows, :])
                gv = gv + m * dy[step, x, rows, :]
            gurow[pl.ds(x, 1), :] = jnp.sum(gu, axis=0, keepdims=True)
            gvrow[pl.ds(x, 1), :] = jnp.sum(gv, axis=0, keepdims=True)
            return packed

        packed = rows_of(gather_body, 1, SUB - 1, zero)
        wait_all(row_copies)
        if step == ITERS - 1:
            h_w = jnp.where(first_row, jnp.broadcast_to(state[step, 0, hrow:hrow + 1, :], (SUB, LANE)), h_w)
            h_e = jnp.where(last_row, jnp.broadcast_to(state[step, SUB + 1, hrow:hrow + 1, :], (SUB, LANE)), h_e)
            brow[step] = (0.25 * ADVECTION) * (h_e - h_w)
        else:
            add_rows(step + 1)
            lam_h = height_arrivals(step + 1, lam_h, columns)
        packed = gather_body(SUB - 1, gather_body(0, packed))
        gu = (-0.25 * ADVECTION) * gurow[...]
        gv = (-0.25 * ADVECTION) * gvrow[...]
        spread_h = HEIGHT_DIFFUSION * lam_h
        to_e, to_w, to_n, to_s = spread_h + gv, spread_h - gv, spread_h - gu, spread_h + gu
        a_last = row_of(arow.at[step], SUB)
        a_first = row_of(arow.at[step], 1)
        for t in range(tiles):
            rows = slice(t * SUB, (t + 1) * SUB)
            slab_s[step, 0, rows, :] = (diff[t] - a_last) * mu[SUB, rows, :]
            slab_s[step, 1, rows, :] = (diff[t] + a_first) * mu[1, rows, :]
        slab_s[step, 0, hrow:hrow + SUB, :] = jnp.broadcast_to(to_e[SUB - 1:SUB, :], (SUB, LANE))
        slab_s[step, 1, hrow:hrow + SUB, :] = jnp.broadcast_to(to_w[0:1, :], (SUB, LANE))
        row_copies = exchange_rows(
            slab_s.at[step, 0], slab_r.at[step, 0], slab_s.at[step, 1], slab_r.at[step, 1], b_send, b_recv, step,
        )
        bpacks[step] = packed_with(packed, jnp.where(last_lane, to_n, to_s), hslot)
        column_copies = exchange_columns(bpacks.at[step], bpackr, b_send, b_recv, step)

        mrow[...] = (BUOYANCY / levels) * wet_tile * lam_h

        def local_body(x, carry):
            a_w = row_of(arow.at[step], x)
            a_e = row_of(arow.at[step], x + 2)
            b = row_of(brow.at[step], x)
            centre = [mu[x + 1, t * SUB:(t + 1) * SUB, :] for t in range(tiles)]
            vert = vertical(centre)
            push = row_of(mrow, x)
            for t in range(tiles):
                rows = slice(t * SUB, (t + 1) * SUB)
                m = centre[t]
                m_w = mu[x, rows, :]
                m_e = mu[x + 2, rows, :]
                bm = b * m
                dm = diff[t] * m
                from_s = jnp.where(first_lane, 0.0, roll_lanes(dm - bm, 1))
                from_n = jnp.where(last_lane, 0.0, roll_lanes(dm + bm, LANE - 1))
                value = lam[x, rows, :] + VERTICAL_MIX * vert[t] - 4.0 * dm + from_s + from_n
                value = value + diff[t] * (m_w + m_e) + (a_e * m_e - a_w * m_w)
                if t < per:
                    value = value + push
                lam[x, rows, :] = value
            return carry

        rows_of(local_body, 0, SUB, 0)
        damp = jnp.tanh(heights[step])
        lam_h = (
            lam_h - 4.0 * spread_h - HEIGHT_DAMPING * (1.0 - damp * damp) * lam_h
            + jnp.where(first_row, 0.0, roll_rows(to_e, 1)) + jnp.where(last_row, 0.0, roll_rows(to_w, SUB - 1))
            + jnp.where(first_lane, 0.0, roll_lanes(to_n, 1)) + jnp.where(last_lane, 0.0, roll_lanes(to_s, LANE - 1))
        )

    wait_all(column_copies)
    columns = unpacked(bpackr, 0)

    def write_row(x):
        for t in range(tiles):
            value = lam[x, t * SUB:(t + 1) * SUB, :] + jnp.where(edge_lane, spread(columns, x * tiles + t), 0.0)
            out_ref[pl.ds(t * SUB * SUB + x, SUB, stride=SUB), :] = value

    for x in range(1, SUB - 1):
        write_row(x)
    wait_all(row_copies)
    add_rows(0)
    write_row(0)
    write_row(SUB - 1)
    outh_ref[...] = height_arrivals(0, lam_h, columns)

    for copy in a2a + sends:
        copy.wait_send()


def local(checkpoint, holder_list, height, land_mask, diffusivity, tracer_weight, height_weight):
    n, n_y = lax.axis_size("gx"), lax.axis_size("gy")
    width_x, width_y = height.shape
    assert (width_x, width_y) == (SUB, LANE)
    levels = diffusivity.shape[1]
    channels = 3 * levels
    piece_rows = checkpoint.shape[3] // LANE
    padded = -(-piece_rows // SUB) * SUB
    rows = channels + SUB
    f32 = jnp.float32
    vmem = pl.BlockSpec(memory_space=pltpu.VMEM)
    tile = pltpu.VMEM((SUB, LANE), f32)
    out, out_h = pl.pallas_call(
        functools.partial(kernel, n, n_y, levels, piece_rows),
        out_shape=(
            jax.ShapeDtypeStruct((channels * SUB, LANE), f32),
            jax.ShapeDtypeStruct((SUB, LANE), f32),
        ),
        in_specs=[pl.BlockSpec(memory_space=pltpu.HBM)] * 7,
        out_specs=(vmem, vmem),
        scratch_shapes=[
            pltpu.VMEM((n * padded, LANE), f32),
            pltpu.VMEM((n, padded, LANE), f32),
            pltpu.VMEM((ITERS, SUB + 2, rows, LANE), f32),
            pltpu.VMEM((ITERS, SUB, channels, LANE), f32),
            pltpu.VMEM((channels * SUB, LANE), f32),
            pltpu.VMEM((SUB, channels, LANE), f32),
            pltpu.VMEM((SUB + 2, channels, LANE), f32),
            tile,
            pltpu.VMEM((ITERS, 2 * SUB, LANE), f32),
            pltpu.VMEM((ITERS, SUB, LANE), f32),
            tile, tile, tile,
            pltpu.VMEM((ITERS, SUB, LANE), f32),
            pltpu.VMEM((ITERS, 2, SUB, LANE), f32),
            pltpu.VMEM((ITERS, 2, rows, LANE), f32),
            pltpu.VMEM((ITERS, 2, rows, LANE), f32),
            pltpu.VMEM((ITERS, SUB, LANE), f32),
            pltpu.VMEM((ITERS, 2, SUB, LANE), f32),
            pltpu.SMEM(holder_list.shape, jnp.int32),
            pltpu.SMEM(diffusivity.shape, f32),
            pltpu.VMEM(checkpoint.shape[2:], f32),
            tile,
            pltpu.VMEM((SUB, LANE), jnp.int32),
            tile,
            pltpu.SemaphoreType.DMA((n,)),
            pltpu.SemaphoreType.DMA((n,)),
            pltpu.SemaphoreType.DMA((ITERS, 4)),
            pltpu.SemaphoreType.DMA((ITERS, 4)),
            pltpu.SemaphoreType.DMA((ITERS, 4)),
            pltpu.SemaphoreType.DMA((ITERS, 4)),
            pltpu.SemaphoreType.DMA((7,)),
        ],
        compiler_params=pltpu.CompilerParams(
            collective_id=0, has_side_effects=True, vmem_limit_bytes=32 * 2**20
        ),
    )(
        holder_list, diffusivity, checkpoint.reshape(checkpoint.shape[2:]), height, land_mask,
        tracer_weight.reshape(channels * SUB, LANE), height_weight,
    )
    return out.reshape(tracer_weight.shape), out_h


def solution(mesh):
    return jax.shard_map(
        local,
        mesh=mesh,
        in_specs=(
            P(("member", "gx"), "gy", None, None),
            P(("member", "gx"), "gy", None),
            P(("member", "gx"), "gy"),
            P("gx", "gy"),
            P(),
            P("member", None, "gx", "gy"),
            P(("member", "gx"), "gy"),
        ),
        out_specs=(P("member", None, "gx", "gy"), P(("member", "gx"), "gy")),
        check_vma=False,
    )
```

```python
import functools
import jax
import jax.numpy as jnp
from jax import lax
from jax.experimental import pallas as pl
from jax.experimental.pallas import tpu as pltpu
from jax.sharding import PartitionSpec as P

ITERS = 4
ADVECTION = 0.3
VERTICAL_MIX = 0.1
HEIGHT_DIFFUSION = 0.2
HEIGHT_DAMPING = 0.3
BUOYANCY = 0.5

SUB = 8
LANE = 128
MESH = pl.DeviceIdType.MESH


def roll_lanes(value, shift):
    return pltpu.roll(value, shift, 1)


def roll_rows(value, shift):
    return pltpu.roll(value, shift, 0)


def kernel(
    n, n_y, levels, piece_rows,
    holder_hbm, diff_hbm, ckpt_hbm, height_hbm, mask_hbm, tw_hbm, hw_hbm,
    out_ref, outh_ref,
    buf, recv, state, dy, tw, lam, mu, wet, arow, brow, mrow, gurow, gvrow,
    packs, packr, dpacks, dpackr, slab_s, slab_r, bpacks, bpackr,
    holder_ref, diff_ref, ckpt_ref, height_ref, mask_ref, hw_ref,
    a2a_send, a2a_recv, f_send, f_recv, b_send, b_recv, in_sem,
):
    me = lax.axis_index("gx")
    my = lax.axis_index("gy")
    east, west = lax.rem(me + 1, n), lax.rem(me + n - 1, n)
    north, south = lax.rem(my + 1, n_y), lax.rem(my + n_y - 1, n_y)
    channels = 3 * levels
    tiles = channels // SUB
    per = levels // SUB
    hrow = channels
    padded = -(-piece_rows // SUB) * SUB

    inputs = (
        (ckpt_hbm, ckpt_ref), (diff_hbm, diff_ref), (mask_hbm, mask_ref), (tw_hbm, tw),
        (height_hbm, height_ref), (hw_hbm, hw_ref), (holder_hbm, holder_ref),
    )
    loads = [pltpu.make_async_copy(source, target, in_sem.at[i]) for i, (source, target) in enumerate(inputs)]
    for load in loads:
        load.start()

    barrier = pltpu.get_barrier_semaphore()
    for k in range(1, n):
        pl.semaphore_signal(barrier, inc=1, device_id={"gx": lax.rem(me + k, n)}, device_id_type=MESH)
    for other in (north, south):
        pl.semaphore_signal(barrier, inc=1, device_id={"gy": other}, device_id_type=MESH)
        for side in (east, west):
            pl.semaphore_signal(barrier, inc=1, device_id={"gx": side, "gy": other}, device_id_type=MESH)

    loads[0].wait()
    depth = 0 if piece_rows % SUB else piece_rows // SUB
    if padded != piece_rows:
        buf[...] = jnp.zeros_like(buf)
    for o in range(0, n, SUB):
        size = min(SUB, n - o)
        for r in range(piece_rows):
            row = r % SUB * depth + r // SUB if depth else r
            buf[pl.ds(o * padded + row, size, stride=padded), :] = ckpt_ref[o:o + size, r * LANE:(r + 1) * LANE]

    pl.semaphore_wait(barrier, n + 5)

    mine = pl.multiple_of(me * padded, SUB)
    sends = []
    a2a = []
    for k in range(1, n):
        owner = lax.rem(me + k, n)
        copy = pltpu.make_async_remote_copy(
            src_ref=buf.at[pl.ds(pl.multiple_of(owner * padded, SUB), padded)],
            dst_ref=recv.at[me],
            send_sem=a2a_send.at[k], recv_sem=a2a_recv.at[k],
            device_id={"gx": owner}, device_id_type=MESH,
        )
        copy.start()
        a2a.append(copy)
    recv[me] = buf[pl.ds(mine, padded), :]

    lane = lax.broadcasted_iota(jnp.int32, (SUB, LANE), 1)
    sub = lax.broadcasted_iota(jnp.int32, (SUB, LANE), 0)
    first_lane, last_lane = lane == 0, lane == LANE - 1
    edge_lane = first_lane | last_lane
    first_row, last_row = sub == 0, sub == SUB - 1
    pair = lax.shift_right_logical(lane, 1)
    even = (lane & 1) == 0
    zero = jnp.zeros((SUB, LANE), jnp.float32)

    for load in loads[1:]:
        load.wait()
    mrow[0:SUB, :] = zero
    mrow[SUB:2 * SUB, :] = zero
    diff = []
    for t in range(tiles):
        value = zero
        for s in range(SUB):
            channel = t * SUB + s
            value = jnp.where(sub == s, diff_ref[channel // levels, channel % levels], value)
        diff.append(value)
    wet_tile = mask_ref[...].astype(jnp.float32)
    wet[1:SUB + 1, :] = wet_tile
    for t in range(tiles):
        rows = pl.ds(t * SUB, SUB)
        mu[0, rows, :] = zero
        mu[SUB + 1, rows, :] = zero
    for t in range(ITERS):
        arow[t, 0:SUB, :] = zero
        arow[t, SUB:2 * SUB, :] = zero
    for x in range(SUB):
        for t in range(tiles):
            lam[x, t * SUB:(t + 1) * SUB, :] = tw[pl.ds(t * SUB * SUB + x, SUB, stride=SUB), :]

    for copy in a2a:
        copy.wait_recv()
    for p in range(n):
        holder = holder_ref[0, 0, p]
        if depth:
            for x in range(SUB):
                state[0, x + 2, p * depth:(p + 1) * depth, :] = recv[holder, x * depth:(x + 1) * depth, :]
        else:
            for r in range(piece_rows):
                row = p * piece_rows + r
                state[0, row % SUB + 2, row // SUB:row // SUB + 1, :] = recv[holder, r:r + 1, :]

    def exchange(route, send_sem, recv_sem, step, first):
        copies = []
        for i, (source, target, device) in enumerate(route, first):
            copy = pltpu.make_async_remote_copy(
                src_ref=source, dst_ref=target, send_sem=send_sem.at[step, i], recv_sem=recv_sem.at[step, i],
                device_id=device, device_id_type=MESH,
            )
            copy.start()
            copies.append(copy)
        sends.extend(copies)
        return copies

    def exchange_rows(send_east, recv_east, send_west, recv_west, send_sem, recv_sem, step):
        route = ((send_east, recv_east, {"gx": east}), (send_west, recv_west, {"gx": west}))
        return exchange(route, send_sem, recv_sem, step, 0)

    def exchange_columns(pack_out, pack_in, send_sem, recv_sem, step):
        route = ((pack_out, pack_in.at[step, 0], {"gy": north}), (pack_out, pack_in.at[step, 1], {"gy": south}))
        return exchange(route, send_sem, recv_sem, step, 2)

    def wait_all(copies):
        for copy in copies:
            copy.wait_recv()

    def rows_of(body, first, last, carry):
        return lax.fori_loop(first, last, body, carry, unroll=3 if (last - first) % 3 == 0 else 4)

    def unpacked(south_value, north_value, distance=1):
        from_south = jnp.where(my > 0, roll_lanes(south_value, distance), zero)
        from_north = jnp.where(my < n_y - 1, roll_lanes(north_value, LANE - distance), zero)
        return jnp.where(even, from_north, from_south)

    def spread(columns, k):
        return roll_lanes(columns, lax.rem(2 * LANE - 1 - 2 * k, LANE))

    def packed_with(packed, value, k):
        return jnp.where(pair == k, roll_lanes(value, 2 * k + 1), packed)

    def vertical(values):
        result = [None] * tiles
        for tracer in range(3):
            group = values[tracer * per:(tracer + 1) * per]
            down = [roll_rows(v, 1) for v in group]
            up = [roll_rows(v, SUB - 1) for v in group]
            for i, v in enumerate(group):
                upper = jnp.where(first_row, down[i - 1] if i else v, down[i])
                lower = jnp.where(last_row, up[i + 1] if i < per - 1 else v, up[i])
                result[tracer * per + i] = upper + lower - 2.0 * v
        return result

    def row_of(ref, x):
        return jnp.broadcast_to(ref[pl.ds(x, 1), :], (SUB, LANE))

    hslot = channels
    width = 2 * tiles
    span = width * SUB
    lead = pair == 0
    for x in range(1, SUB):
        lead = lead | (pair == x * tiles)
    strip_diff = zero
    for t in range(tiles):
        strip_diff = strip_diff + diff[t] * roll_lanes(jnp.where(lead, 1.0, 0.0), 2 * t)
    inside = (jnp.where(even, n_y - 1 - my, my) > 0) & (lane < span)
    top_tile = (pair & (per - 1)) == 0
    low_tile = (pair & (per - 1)) == per - 1

    def whole_row(value, x):
        return jnp.broadcast_to(value[x:x + 1, :], (SUB, LANE))

    def repeated(value):
        value = value + roll_lanes(value, 2)
        return value + roll_lanes(value, 4) + roll_lanes(value, 8)

    def row_strips(value):
        near, far = zero, zero
        for x in range(SUB):
            k = x * tiles
            moved = roll_lanes(whole_row(value, x), 2 * k + 1)
            near = jnp.where(pair == k, moved, near)
            far = jnp.where((lane == (2 * k + LANE - 1) % LANE) | (lane == 2 * k + 2), moved, far)
        return repeated(near), repeated(far)

    def send_rows(step, h):
        for x in (0, 1, SUB - 2, SUB - 1):
            state[step, x + 2, hrow:hrow + SUB, :] = jnp.where(sub < SUB // 2, whole_row(h, x), whole_row(wet_tile, x))
        return exchange_rows(
            state.at[step, pl.ds(SUB, 2)], state.at[step, pl.ds(0, 2)],
            state.at[step, pl.ds(2, 2)], state.at[step, pl.ds(SUB + 2, 2)], f_send, f_recv, step,
        )

    def send_corners(step, packed, h):
        dpacks[step, 0] = packed_with(packed, h, hslot)
        dpacks[step, 1] = row_strips(h)[0]
        route = []
        for i, (x_to, y_to) in enumerate(((east, north), (east, south), (west, north), (west, south))):
            route.append((dpacks.at[step], dpackr.at[step, i], {"gx": x_to, "gy": y_to}))
        return exchange(route, f_send, f_recv, step, 4)

    def send_columns(step, packed, far, h):
        packs[step, 0] = packed_with(packed, h, hslot)
        packs[step, 1] = far
        packs[step, 2], packs[step, 3] = row_strips(h)
        packs[step, 4] = wet_near
        return exchange_columns(packs.at[step], packr, f_send, f_recv, step)

    def pack_row(value, k, packed):
        near, far = packed
        moved = roll_lanes(value, 2 * k + 1)
        before, after = lax.rem(2 * k + LANE - 1, LANE), 2 * k + 2
        return jnp.where(pair == k, moved, near), jnp.where((lane == before) | (lane == after), moved, far)

    def pack_body(x, packed):
        for t in range(tiles):
            packed = pack_row(state[0, x + 2, t * SUB:(t + 1) * SUB, :], x * tiles + t, packed)
        return packed

    wet_near = row_strips(wet_tile)[0]
    heights = [height_ref[...]]
    row_copies = send_rows(0, heights[0])
    packed = pack_body(SUB - 1, pack_body(0, (zero, zero)))
    corner_copies = send_corners(0, packed[0], heights[0])
    packed = rows_of(pack_body, 1, SUB - 1, packed)
    column_copies = send_columns(0, packed[0], packed[1], heights[0])
    strip_wet = None

    def forward_row(step, x, k, columns, packed, update, own):
        a = row_of(arow.at[step], x + 1)
        b = row_of(brow.at[step], x + 1)
        w = row_of(wet, x + 1)
        centre = [state[step, x + 2, t * SUB:(t + 1) * SUB, :] for t in range(tiles)]
        if update:
            vert = vertical(centre)
            total = centre[0]
            for i in range(1, per):
                total = total + centre[i]
            mrow[pl.ds(x + 1, 1), :] = jnp.sum(total, axis=0, keepdims=True)
        for t in range(tiles):
            rows = slice(t * SUB, (t + 1) * SUB)
            c = centre[t]
            side = spread(columns, k + t)
            c_s = jnp.where(first_lane, side, roll_lanes(c, 1))
            c_n = jnp.where(last_lane, side, roll_lanes(c, LANE - 1))
            delta = c_n - c_s
            if own:
                dy[step, x, rows, :] = delta
            if update:
                c_e = state[step, x + 3, rows, :]
                c_w = state[step, x + 1, rows, :]
                lap = c_e + c_w + c_n + c_s - 4.0 * c
                new = c + w * (diff[t] * lap - a * (c_e - c_w) - b * delta + VERTICAL_MIX * vert[t])
                state[step + 1, x + 2, rows, :] = new
                if packed is not None:
                    packed = pack_row(new, k + t, packed)
        return packed

    def next_height(h, h_e, h_w, h_n, h_s, w, total):
        lap = h_e + h_w + h_n + h_s - 4.0 * h
        return h + HEIGHT_DIFFUSION * lap - HEIGHT_DAMPING * jnp.tanh(h) + (BUOYANCY / levels) * w * total

    def along_latitude(h, side):
        h_n = jnp.where(last_lane, side, roll_lanes(h, LANE - 1))
        h_s = jnp.where(first_lane, side, roll_lanes(h, 1))
        return h_n, h_s

    for step in range(0, ITERS, 2):
        h = heights[step]
        wait_all(column_copies)
        received = [
            unpacked(packr[step, 0, slot], packr[step, 1, slot], distance)
            for slot, distance in ((0, 1), (1, 2), (2, 1), (3, 2), (4, 1))
        ]
        columns, far_columns, strip_h, far_h, strip_w = received
        strip_wet = strip_w if step == 0 else strip_wet
        h_n, h_s = along_latitude(h, spread(columns, hslot))
        h_w, h_e = roll_rows(h, 1), roll_rows(h, SUB - 1)
        arow[step, 1:SUB + 1, :] = (-0.25 * ADVECTION) * (h_n - h_s)
        brow[step, 1:SUB + 1, :] = (0.25 * ADVECTION) * (h_e - h_w)

        def inner_body(x, carry):
            forward_row(step, x, x * tiles, columns, None, True, True)
            return carry

        rows_of(inner_body, 1, SUB - 1, 0)
        wait_all(row_copies)
        wait_all(corner_copies)
        corner_w, corner_e = (unpacked(dpackr[step, i, 0], dpackr[step, i + 1, 0]) for i in (0, 2))
        corner_hw, corner_he = (unpacked(dpackr[step, i, 1], dpackr[step, i + 1, 1]) for i in (0, 2))
        ring = []
        for x, far_x, near, corner, row in (
            (-1, 0, 0, corner_w, SUB - 1), (SUB, SUB + 3, SUB - 1, corner_e, 0),
        ):
            h_ring = jnp.broadcast_to(state[step, x + 2, hrow:hrow + 1, :], (SUB, LANE))
            h_out = jnp.broadcast_to(state[step, far_x, hrow:hrow + 1, :], (SUB, LANE))
            h_in = whole_row(h, near)
            if step == 0:
                wet[x + 1:x + 2, :] = state[step, x + 2, hrow + SUB // 2:hrow + SUB // 2 + 1, :]
            ring_n, ring_s = along_latitude(h_ring, whole_row(spread(corner, hslot), row))
            ring_e, ring_w = (h_in, h_out) if x < 0 else (h_out, h_in)
            arow[step, x + 1:x + 2, :] = ((-0.25 * ADVECTION) * (ring_n - ring_s))[0:1, :]
            brow[step, x + 1:x + 2, :] = ((0.25 * ADVECTION) * (ring_e - ring_w))[0:1, :]
            forward_row(step, x, row * tiles, corner, None, True, False)
            ring.append((
                h_ring, next_height(h_ring, ring_e, ring_w, ring_n, ring_s, row_of(wet, x + 1), row_of(mrow, x + 1)),
            ))
        h_w = jnp.where(first_row, ring[0][0], h_w)
        h_e = jnp.where(last_row, ring[1][0], h_e)
        brow[step, 1:SUB + 1, :] = (0.25 * ADVECTION) * (h_e - h_w)
        for x in (0, SUB - 1):
            forward_row(step, x, x * tiles, columns, None, True, True)
        h_next = next_height(h, h_e, h_w, h_n, h_s, wet_tile, mrow[1:SUB + 1, :])

        def strip_sides(value, from_e, from_w):
            e = jnp.where(lane >= span - width, roll_lanes(from_e, span - width), roll_lanes(value, LANE - width))
            w = jnp.where(lane < width, roll_lanes(from_w, LANE - span + width), roll_lanes(value, width))
            return e, w

        own = packs[step, 0]
        own_h = packs[step, 2]
        c_e, c_w = strip_sides(columns, corner_e, corner_w)
        c_n, c_s = jnp.where(even, far_columns, own), jnp.where(even, own, far_columns)
        s_e, s_w = strip_sides(strip_h, corner_he, corner_hw)
        s_n, s_s = jnp.where(even, far_h, own_h), jnp.where(even, own_h, far_h)
        down, up = roll_rows(columns, 1), roll_rows(columns, SUB - 1)
        upper = jnp.where(first_row, jnp.where(top_tile, columns, roll_lanes(down, 2)), down)
        lower = jnp.where(last_row, jnp.where(low_tile, columns, roll_lanes(up, LANE - 2)), up)
        a = (-0.25 * ADVECTION) * (s_n - s_s)
        b = (0.25 * ADVECTION) * (s_e - s_w)
        lap = c_e + c_w + c_n + c_s - 4.0 * columns
        strip = columns + strip_wet * (
            strip_diff * lap - a * (c_e - c_w) - b * (c_n - c_s) + VERTICAL_MIX * (upper + lower - 2.0 * columns)
        )
        sums = jnp.broadcast_to(jnp.sum(columns, axis=0, keepdims=True), (SUB, LANE))
        total = sums
        for i in range(1, per):
            total = total + roll_lanes(sums, LANE - 2 * i)
        total = repeated(jnp.where(lead, total, 0.0))
        strip_h = next_height(strip_h, s_e, s_w, s_n, s_s, strip_wet, total)
        columns = jnp.where(inside, strip, 0.0)
        strip_h = jnp.where(inside, strip_h, 0.0)
        side = zero
        for x in range(SUB):
            side = jnp.where(sub == x, spread(strip_h, x * tiles), side)

        step += 1
        final = step == ITERS - 1
        h = h_next
        heights.append(h)
        h_n, h_s = along_latitude(h, side)
        h_w = jnp.where(first_row, ring[0][1], roll_rows(h, 1))
        h_e = jnp.where(last_row, ring[1][1], roll_rows(h, SUB - 1))
        arow[step, 1:SUB + 1, :] = (-0.25 * ADVECTION) * (h_n - h_s)
        brow[step, 1:SUB + 1, :] = (0.25 * ADVECTION) * (h_e - h_w)

        def second_body(x, packed):
            done = forward_row(step, x, x * tiles, columns, None if final else packed, not final, True)
            return packed if final else done

        if final:
            rows_of(second_body, 0, SUB, 0)
            break
        packed = (zero, zero)
        for x in (0, 1, SUB - 2, SUB - 1):
            packed = second_body(x, packed)
        h_edges = next_height(h, h_e, h_w, h_n, h_s, wet_tile, mrow[1:SUB + 1, :])
        row_copies = send_rows(step + 1, h_edges)
        corner_copies = send_corners(step + 1, packed[0], h_edges)
        packed = rows_of(second_body, 2, SUB - 2, packed)
        h = next_height(h, h_e, h_w, h_n, h_s, wet_tile, mrow[1:SUB + 1, :])
        heights.append(h)
        column_copies = send_columns(step + 1, packed[0], packed[1], h)

    def add_rows(step):
        for t in range(tiles):
            rows = slice(t * SUB, (t + 1) * SUB)
            lam[0, rows, :] = lam[0, rows, :] + slab_r[step, 0, rows, :]
            lam[SUB - 1, rows, :] = lam[SUB - 1, rows, :] + slab_r[step, 1, rows, :]

    def height_arrivals(step, lam_h, columns):
        lam_h = lam_h + jnp.where(edge_lane, spread(columns, hslot), 0.0)
        lam_h = lam_h + jnp.where(first_row, jnp.broadcast_to(slab_r[step, 0, hrow:hrow + 1, :], (SUB, LANE)), 0.0)
        return lam_h + jnp.where(last_row, jnp.broadcast_to(slab_r[step, 1, hrow:hrow + 1, :], (SUB, LANE)), 0.0)

    lam_h = hw_ref[...]
    columns = None
    for step in reversed(range(ITERS)):
        if step < ITERS - 1:
            wait_all(column_copies)
            columns = unpacked(bpackr[step + 1, 0], bpackr[step + 1, 1])

        def gather_body(x, packed):
            b = row_of(brow.at[step], x + 1)
            w = row_of(wet, x + 1)
            gu = zero
            gv = zero
            for t in range(tiles):
                rows = slice(t * SUB, (t + 1) * SUB)
                value = lam[x, rows, :]
                if columns is not None:
                    value = value + jnp.where(edge_lane, spread(columns, x * tiles + t), 0.0)
                    lam[x, rows, :] = value
                m = w * value
                mu[x + 1, rows, :] = m
                bm = b * m
                dm = diff[t] * m
                packed = packed_with(packed, jnp.where(last_lane, dm - bm, dm + bm), x * tiles + t)
                gu = gu + m * (state[step, x + 3, rows, :] - state[step, x + 1, rows, :])
                gv = gv + m * dy[step, x, rows, :]
            gurow[pl.ds(x, 1), :] = jnp.sum(gu, axis=0, keepdims=True)
            gvrow[pl.ds(x, 1), :] = jnp.sum(gv, axis=0, keepdims=True)
            return packed

        packed = rows_of(gather_body, 1, SUB - 1, zero)
        if step < ITERS - 1:
            wait_all(row_copies)
            add_rows(step + 1)
            lam_h = height_arrivals(step + 1, lam_h, columns)
        packed = gather_body(SUB - 1, gather_body(0, packed))
        gu = (-0.25 * ADVECTION) * gurow[...]
        gv = (-0.25 * ADVECTION) * gvrow[...]
        spread_h = HEIGHT_DIFFUSION * lam_h
        to_e, to_w, to_n, to_s = spread_h + gv, spread_h - gv, spread_h - gu, spread_h + gu
        a_last = row_of(arow.at[step], SUB)
        a_first = row_of(arow.at[step], 1)
        for t in range(tiles):
            rows = slice(t * SUB, (t + 1) * SUB)
            slab_s[step, 0, rows, :] = (diff[t] - a_last) * mu[SUB, rows, :]
            slab_s[step, 1, rows, :] = (diff[t] + a_first) * mu[1, rows, :]
        slab_s[step, 0, hrow:hrow + SUB, :] = jnp.broadcast_to(to_e[SUB - 1:SUB, :], (SUB, LANE))
        slab_s[step, 1, hrow:hrow + SUB, :] = jnp.broadcast_to(to_w[0:1, :], (SUB, LANE))
        row_copies = exchange_rows(
            slab_s.at[step, 0], slab_r.at[step, 0], slab_s.at[step, 1], slab_r.at[step, 1], b_send, b_recv, step,
        )
        bpacks[step] = packed_with(packed, jnp.where(last_lane, to_n, to_s), hslot)
        column_copies = exchange_columns(bpacks.at[step], bpackr, b_send, b_recv, step)

        mrow[0:SUB, :] = (BUOYANCY / levels) * wet_tile * lam_h

        def local_body(x, carry):
            a_w = row_of(arow.at[step], x)
            a_e = row_of(arow.at[step], x + 2)
            b = row_of(brow.at[step], x + 1)
            centre = [mu[x + 1, t * SUB:(t + 1) * SUB, :] for t in range(tiles)]
            vert = vertical(centre)
            push = row_of(mrow, x)
            for t in range(tiles):
                rows = slice(t * SUB, (t + 1) * SUB)
                m = centre[t]
                m_w = mu[x, rows, :]
                m_e = mu[x + 2, rows, :]
                bm = b * m
                dm = diff[t] * m
                from_s = jnp.where(first_lane, 0.0, roll_lanes(dm - bm, 1))
                from_n = jnp.where(last_lane, 0.0, roll_lanes(dm + bm, LANE - 1))
                value = lam[x, rows, :] + VERTICAL_MIX * vert[t] - 4.0 * dm + from_s + from_n
                value = value + diff[t] * (m_w + m_e) + (a_e * m_e - a_w * m_w)
                if t < per:
                    value = value + push
                lam[x, rows, :] = value
            return carry

        rows_of(local_body, 0, SUB, 0)
        damp = jnp.tanh(heights[step])
        lam_h = (
            lam_h - 4.0 * spread_h - HEIGHT_DAMPING * (1.0 - damp * damp) * lam_h
            + jnp.where(first_row, 0.0, roll_rows(to_e, 1)) + jnp.where(last_row, 0.0, roll_rows(to_w, SUB - 1))
            + jnp.where(first_lane, 0.0, roll_lanes(to_n, 1)) + jnp.where(last_lane, 0.0, roll_lanes(to_s, LANE - 1))
        )

    wait_all(column_copies)
    columns = unpacked(bpackr[0, 0], bpackr[0, 1])

    def write_row(x):
        for t in range(tiles):
            value = lam[x, t * SUB:(t + 1) * SUB, :] + jnp.where(edge_lane, spread(columns, x * tiles + t), 0.0)
            out_ref[pl.ds(t * SUB * SUB + x, SUB, stride=SUB), :] = value

    for x in range(1, SUB - 1):
        write_row(x)
    wait_all(row_copies)
    add_rows(0)
    write_row(0)
    write_row(SUB - 1)
    outh_ref[...] = height_arrivals(0, lam_h, columns)

    for copy in a2a + sends:
        copy.wait_send()


def local(checkpoint, holder_list, height, land_mask, diffusivity, tracer_weight, height_weight):
    n, n_y = lax.axis_size("gx"), lax.axis_size("gy")
    width_x, width_y = height.shape
    assert (width_x, width_y) == (SUB, LANE)
    levels = diffusivity.shape[1]
    channels = 3 * levels
    piece_rows = checkpoint.shape[3] // LANE
    padded = -(-piece_rows // SUB) * SUB
    rows = channels + SUB
    f32 = jnp.float32
    vmem = pl.BlockSpec(memory_space=pltpu.VMEM)
    tile = pltpu.VMEM((SUB, LANE), f32)
    out, out_h = pl.pallas_call(
        functools.partial(kernel, n, n_y, levels, piece_rows),
        out_shape=(
            jax.ShapeDtypeStruct((channels * SUB, LANE), f32),
            jax.ShapeDtypeStruct((SUB, LANE), f32),
        ),
        in_specs=[pl.BlockSpec(memory_space=pltpu.HBM)] * 7,
        out_specs=(vmem, vmem),
        scratch_shapes=[
            pltpu.VMEM((n * padded, LANE), f32),
            pltpu.VMEM((n, padded, LANE), f32),
            pltpu.VMEM((ITERS, SUB + 4, rows, LANE), f32),
            pltpu.VMEM((ITERS, SUB, channels, LANE), f32),
            pltpu.VMEM((channels * SUB, LANE), f32),
            pltpu.VMEM((SUB, channels, LANE), f32),
            pltpu.VMEM((SUB + 2, channels, LANE), f32),
            pltpu.VMEM((2 * SUB, LANE), f32),
            pltpu.VMEM((ITERS, 2 * SUB, LANE), f32),
            pltpu.VMEM((ITERS, 2 * SUB, LANE), f32),
            pltpu.VMEM((2 * SUB, LANE), f32),
            tile, tile,
            pltpu.VMEM((ITERS, 5, SUB, LANE), f32),
            pltpu.VMEM((ITERS, 2, 5, SUB, LANE), f32),
            pltpu.VMEM((ITERS, 2, SUB, LANE), f32),
            pltpu.VMEM((ITERS, 4, 2, SUB, LANE), f32),
            pltpu.VMEM((ITERS, 2, rows, LANE), f32),
            pltpu.VMEM((ITERS, 2, rows, LANE), f32),
            pltpu.VMEM((ITERS, SUB, LANE), f32),
            pltpu.VMEM((ITERS, 2, SUB, LANE), f32),
            pltpu.SMEM(holder_list.shape, jnp.int32),
            pltpu.SMEM(diffusivity.shape, f32),
            pltpu.VMEM(checkpoint.shape[2:], f32),
            tile,
            pltpu.VMEM((SUB, LANE), jnp.int32),
            tile,
            pltpu.SemaphoreType.DMA((n,)),
            pltpu.SemaphoreType.DMA((n,)),
            pltpu.SemaphoreType.DMA((ITERS, 8)),
            pltpu.SemaphoreType.DMA((ITERS, 8)),
            pltpu.SemaphoreType.DMA((ITERS, 4)),
            pltpu.SemaphoreType.DMA((ITERS, 4)),
            pltpu.SemaphoreType.DMA((7,)),
        ],
        compiler_params=pltpu.CompilerParams(
            collective_id=0, has_side_effects=True, vmem_limit_bytes=60 * 2**20
        ),
    )(
        holder_list, diffusivity, checkpoint.reshape(checkpoint.shape[2:]), height, land_mask,
        tracer_weight.reshape(channels * SUB, LANE), height_weight,
    )
    return out.reshape(tracer_weight.shape), out_h


def solution(mesh):
    return jax.shard_map(
        local,
        mesh=mesh,
        in_specs=(
            P(("member", "gx"), "gy", None, None),
            P(("member", "gx"), "gy", None),
            P(("member", "gx"), "gy"),
            P("gx", "gy"),
            P(),
            P("member", None, "gx", "gy"),
            P(("member", "gx"), "gy"),
        ),
        out_specs=(P("member", None, "gx", "gy"), P(("member", "gx"), "gy")),
        check_vma=False,
    )
```

```python
import functools
import jax
import jax.numpy as jnp
from jax import lax
from jax.experimental import pallas as pl
from jax.experimental.pallas import tpu as pltpu
from jax.sharding import PartitionSpec as P

ITERS = 4
ADVECTION = 0.3
VERTICAL_MIX = 0.1
HEIGHT_DIFFUSION = 0.2
HEIGHT_DAMPING = 0.3
BUOYANCY = 0.5

SUB = 8
LANE = 128
MESH = pl.DeviceIdType.MESH


def roll_lanes(value, shift):
    return pltpu.roll(value, shift, 1)


def roll_rows(value, shift):
    return pltpu.roll(value, shift, 0)


def kernel(
    n, n_y, levels, piece_rows,
    holder_hbm, diff_hbm, ckpt_hbm, height_hbm, mask_hbm, tw_hbm, hw_hbm,
    out_ref, outh_ref,
    buf, recv, state, dy, tw, lam, mu, wet, arow, brow, mrow, gurow, gvrow,
    packs, packr, dpacks, dpackr, slab_s, slab_r, bpacks, bpackr,
    holder_ref, diff_ref, ckpt_ref, height_ref, mask_ref, hw_ref,
    a2a_send, a2a_recv, f_send, f_recv, b_send, b_recv, in_sem,
):
    me = lax.axis_index("gx")
    my = lax.axis_index("gy")
    east, west = lax.rem(me + 1, n), lax.rem(me + n - 1, n)
    north, south = lax.rem(my + 1, n_y), lax.rem(my + n_y - 1, n_y)
    channels = 3 * levels
    tiles = channels // SUB
    per = levels // SUB
    hrow = channels
    padded = -(-piece_rows // SUB) * SUB

    inputs = (
        (ckpt_hbm, ckpt_ref), (diff_hbm, diff_ref), (mask_hbm, mask_ref), (tw_hbm, tw),
        (height_hbm, height_ref), (hw_hbm, hw_ref), (holder_hbm, holder_ref),
    )
    loads = [pltpu.make_async_copy(source, target, in_sem.at[i]) for i, (source, target) in enumerate(inputs)]
    for load in loads:
        load.start()

    barrier = pltpu.get_barrier_semaphore()
    for k in range(1, n):
        pl.semaphore_signal(barrier, inc=1, device_id={"gx": lax.rem(me + k, n)}, device_id_type=MESH)
    for other in (north, south):
        pl.semaphore_signal(barrier, inc=1, device_id={"gy": other}, device_id_type=MESH)
        for side in (east, west):
            pl.semaphore_signal(barrier, inc=1, device_id={"gx": side, "gy": other}, device_id_type=MESH)

    loads[0].wait()
    depth = 0 if piece_rows % SUB else piece_rows // SUB
    if padded != piece_rows:
        buf[...] = jnp.zeros_like(buf)
    for o in range(0, n, SUB):
        size = min(SUB, n - o)
        for r in range(piece_rows):
            row = r % SUB * depth + r // SUB if depth else r
            buf[pl.ds(o * padded + row, size, stride=padded), :] = ckpt_ref[o:o + size, r * LANE:(r + 1) * LANE]

    pl.semaphore_wait(barrier, n + 5)

    mine = pl.multiple_of(me * padded, SUB)
    sends = []
    a2a = []
    for k in range(1, n):
        owner = lax.rem(me + k, n)
        copy = pltpu.make_async_remote_copy(
            src_ref=buf.at[pl.ds(pl.multiple_of(owner * padded, SUB), padded)],
            dst_ref=recv.at[me],
            send_sem=a2a_send.at[k], recv_sem=a2a_recv.at[k],
            device_id={"gx": owner}, device_id_type=MESH,
        )
        copy.start()
        a2a.append(copy)
    recv[me] = buf[pl.ds(mine, padded), :]

    lane = lax.broadcasted_iota(jnp.int32, (SUB, LANE), 1)
    sub = lax.broadcasted_iota(jnp.int32, (SUB, LANE), 0)
    first_lane, last_lane = lane == 0, lane == LANE - 1
    edge_lane = first_lane | last_lane
    first_row, last_row = sub == 0, sub == SUB - 1
    pair = lax.shift_right_logical(lane, 1)
    even = (lane & 1) == 0
    zero = jnp.zeros((SUB, LANE), jnp.float32)

    for load in loads[1:]:
        load.wait()
    gurow[...] = zero
    gvrow[...] = zero
    mrow[0:SUB, :] = zero
    mrow[SUB:2 * SUB, :] = zero
    diff = []
    for t in range(tiles):
        value = zero
        for s in range(SUB):
            channel = t * SUB + s
            value = jnp.where(sub == s, diff_ref[channel // levels, channel % levels], value)
        diff.append(value)
    wet_tile = mask_ref[...].astype(jnp.float32)
    wet[1:SUB + 1, :] = wet_tile
    for t in range(tiles):
        rows = pl.ds(t * SUB, SUB)
        mu[0, rows, :] = zero
        mu[SUB + 1, rows, :] = zero
    for t in range(ITERS):
        arow[t, 0:SUB, :] = zero
        arow[t, SUB:2 * SUB, :] = zero
    for x in range(SUB):
        for t in range(tiles):
            lam[x, t * SUB:(t + 1) * SUB, :] = tw[pl.ds(t * SUB * SUB + x, SUB, stride=SUB), :]

    for copy in a2a:
        copy.wait_recv()
    for p in range(n):
        holder = holder_ref[0, 0, p]
        if depth:
            for x in range(SUB):
                state[0, x + 2, p * depth:(p + 1) * depth, :] = recv[holder, x * depth:(x + 1) * depth, :]
        else:
            for r in range(piece_rows):
                row = p * piece_rows + r
                state[0, row % SUB + 2, row // SUB:row // SUB + 1, :] = recv[holder, r:r + 1, :]

    def exchange(route, send_sem, recv_sem, step, first):
        copies = []
        for i, (source, target, device) in enumerate(route, first):
            copy = pltpu.make_async_remote_copy(
                src_ref=source, dst_ref=target, send_sem=send_sem.at[step, i], recv_sem=recv_sem.at[step, i],
                device_id=device, device_id_type=MESH,
            )
            copy.start()
            copies.append(copy)
        sends.extend(copies)
        return copies

    def exchange_rows(send_east, recv_east, send_west, recv_west, send_sem, recv_sem, step):
        route = ((send_east, recv_east, {"gx": east}), (send_west, recv_west, {"gx": west}))
        return exchange(route, send_sem, recv_sem, step, 0)

    def exchange_columns(pack_out, pack_in, send_sem, recv_sem, step):
        route = ((pack_out, pack_in.at[step, 0], {"gy": north}), (pack_out, pack_in.at[step, 1], {"gy": south}))
        return exchange(route, send_sem, recv_sem, step, 2)

    def wait_all(copies):
        for copy in copies:
            copy.wait_recv()

    def rows_of(body, first, last, carry):
        return lax.fori_loop(first, last, body, carry, unroll=3 if (last - first) % 3 == 0 else 4)

    def unpacked(south_value, north_value, distance=1):
        from_south = jnp.where(my > 0, roll_lanes(south_value, distance), zero)
        from_north = jnp.where(my < n_y - 1, roll_lanes(north_value, LANE - distance), zero)
        return jnp.where(even, from_north, from_south)

    def spread(columns, k):
        return roll_lanes(columns, lax.rem(2 * LANE - 1 - 2 * k, LANE))

    def packed_with(packed, value, k):
        return jnp.where(pair == k, roll_lanes(value, 2 * k + 1), packed)

    def vertical(values):
        result = [None] * tiles
        for tracer in range(3):
            group = values[tracer * per:(tracer + 1) * per]
            down = [roll_rows(v, 1) for v in group]
            up = [roll_rows(v, SUB - 1) for v in group]
            for i, v in enumerate(group):
                upper = jnp.where(first_row, down[i - 1] if i else v, down[i])
                lower = jnp.where(last_row, up[i + 1] if i < per - 1 else v, up[i])
                result[tracer * per + i] = upper + lower - 2.0 * v
        return result

    def row_of(ref, x):
        return jnp.broadcast_to(ref[pl.ds(x, 1), :], (SUB, LANE))

    hslot = channels
    width = 2 * tiles
    span = width * SUB
    lead = pair == 0
    for x in range(1, SUB):
        lead = lead | (pair == x * tiles)
    strip_diff = zero
    for t in range(tiles):
        strip_diff = strip_diff + diff[t] * roll_lanes(jnp.where(lead, 1.0, 0.0), 2 * t)
    inside = (jnp.where(even, n_y - 1 - my, my) > 0) & (lane < span)
    top_tile = (pair & (per - 1)) == 0
    low_tile = (pair & (per - 1)) == per - 1

    def whole_row(value, x):
        return jnp.broadcast_to(value[x:x + 1, :], (SUB, LANE))

    def repeated(value):
        value = value + roll_lanes(value, 2)
        return value + roll_lanes(value, 4) + roll_lanes(value, 8)

    def row_strips(value):
        near, far = zero, zero
        for x in range(SUB):
            k = x * tiles
            moved = roll_lanes(whole_row(value, x), 2 * k + 1)
            near = jnp.where(pair == k, moved, near)
            far = jnp.where((lane == (2 * k + LANE - 1) % LANE) | (lane == 2 * k + 2), moved, far)
        return repeated(near), repeated(far)

    def send_rows(step, h):
        for x in (0, 1, SUB - 2, SUB - 1):
            state[step, x + 2, hrow:hrow + SUB, :] = jnp.where(sub < SUB // 2, whole_row(h, x), whole_row(wet_tile, x))
        return exchange_rows(
            state.at[step, pl.ds(SUB, 2)], state.at[step, pl.ds(0, 2)],
            state.at[step, pl.ds(2, 2)], state.at[step, pl.ds(SUB + 2, 2)], f_send, f_recv, step,
        )

    def send_corners(step, packed, h):
        dpacks[step, 0] = packed_with(packed, h, hslot)
        dpacks[step, 1] = row_strips(h)[0]
        route = []
        for i, (x_to, y_to) in enumerate(((east, north), (east, south), (west, north), (west, south))):
            route.append((dpacks.at[step], dpackr.at[step, i], {"gx": x_to, "gy": y_to}))
        return exchange(route, f_send, f_recv, step, 4)

    def send_columns(step, packed, far, h):
        packs[step, 0] = packed_with(packed, h, hslot)
        packs[step, 1] = far
        packs[step, 2], packs[step, 3] = row_strips(h)
        packs[step, 4] = wet_near
        return exchange_columns(packs.at[step], packr, f_send, f_recv, step)

    def pack_row(value, k, packed):
        near, far = packed
        moved = roll_lanes(value, 2 * k + 1)
        before, after = lax.rem(2 * k + LANE - 1, LANE), 2 * k + 2
        return jnp.where(pair == k, moved, near), jnp.where((lane == before) | (lane == after), moved, far)

    def pack_body(x, packed):
        for t in range(tiles):
            packed = pack_row(state[0, x + 2, t * SUB:(t + 1) * SUB, :], x * tiles + t, packed)
        return packed

    wet_near = row_strips(wet_tile)[0]
    heights = [height_ref[...]]
    row_copies = send_rows(0, heights[0])
    packed = pack_body(SUB - 1, pack_body(0, (zero, zero)))
    corner_copies = send_corners(0, packed[0], heights[0])
    packed = rows_of(pack_body, 1, SUB - 1, packed)
    column_copies = send_columns(0, packed[0], packed[1], heights[0])
    strip_wet = None

    def forward_row(step, x, k, columns, packed, update, own):
        a = row_of(arow.at[step], x + 1)
        b = row_of(brow.at[step], x + 1)
        w = row_of(wet, x + 1)
        centre = [state[step, x + 2, t * SUB:(t + 1) * SUB, :] for t in range(tiles)]
        if update:
            vert = vertical(centre)
            total = centre[0]
            for i in range(1, per):
                total = total + centre[i]
            mrow[pl.ds(x + 1, 1), :] = jnp.sum(total, axis=0, keepdims=True)
        for t in range(tiles):
            rows = slice(t * SUB, (t + 1) * SUB)
            c = centre[t]
            side = spread(columns, k + t)
            c_s = jnp.where(first_lane, side, roll_lanes(c, 1))
            c_n = jnp.where(last_lane, side, roll_lanes(c, LANE - 1))
            delta = c_n - c_s
            if own:
                dy[step, x, rows, :] = delta
            if update:
                c_e = state[step, x + 3, rows, :]
                c_w = state[step, x + 1, rows, :]
                lap = c_e + c_w + c_n + c_s - 4.0 * c
                new = c + w * (diff[t] * lap - a * (c_e - c_w) - b * delta + VERTICAL_MIX * vert[t])
                state[step + 1, x + 2, rows, :] = new
                if packed is not None:
                    packed = pack_row(new, k + t, packed)
        return packed

    def next_height(h, h_e, h_w, h_n, h_s, w, total):
        lap = h_e + h_w + h_n + h_s - 4.0 * h
        return h + HEIGHT_DIFFUSION * lap - HEIGHT_DAMPING * jnp.tanh(h) + (BUOYANCY / levels) * w * total

    def along_latitude(h, side):
        h_n = jnp.where(last_lane, side, roll_lanes(h, LANE - 1))
        h_s = jnp.where(first_lane, side, roll_lanes(h, 1))
        return h_n, h_s

    for step in range(0, ITERS, 2):
        h = heights[step]
        wait_all(column_copies)
        received = [
            unpacked(packr[step, 0, slot], packr[step, 1, slot], distance)
            for slot, distance in ((0, 1), (1, 2), (2, 1), (3, 2), (4, 1))
        ]
        columns, far_columns, strip_h, far_h, strip_w = received
        strip_wet = strip_w if step == 0 else strip_wet
        h_n, h_s = along_latitude(h, spread(columns, hslot))
        h_w, h_e = roll_rows(h, 1), roll_rows(h, SUB - 1)
        arow[step, 1:SUB + 1, :] = (-0.25 * ADVECTION) * (h_n - h_s)
        brow[step, 1:SUB + 1, :] = (0.25 * ADVECTION) * (h_e - h_w)

        def inner_body(x, carry):
            forward_row(step, x, x * tiles, columns, None, True, True)
            return carry

        rows_of(inner_body, 1, SUB - 1, 0)
        wait_all(row_copies)
        wait_all(corner_copies)
        corner_w, corner_e = (unpacked(dpackr[step, i, 0], dpackr[step, i + 1, 0]) for i in (0, 2))
        corner_hw, corner_he = (unpacked(dpackr[step, i, 1], dpackr[step, i + 1, 1]) for i in (0, 2))
        ring = []
        for x, far_x, near, corner, row in (
            (-1, 0, 0, corner_w, SUB - 1), (SUB, SUB + 3, SUB - 1, corner_e, 0),
        ):
            h_ring = jnp.broadcast_to(state[step, x + 2, hrow:hrow + 1, :], (SUB, LANE))
            h_out = jnp.broadcast_to(state[step, far_x, hrow:hrow + 1, :], (SUB, LANE))
            h_in = whole_row(h, near)
            if step == 0:
                wet[x + 1:x + 2, :] = state[step, x + 2, hrow + SUB // 2:hrow + SUB // 2 + 1, :]
            ring_n, ring_s = along_latitude(h_ring, whole_row(spread(corner, hslot), row))
            ring_e, ring_w = (h_in, h_out) if x < 0 else (h_out, h_in)
            arow[step, x + 1:x + 2, :] = ((-0.25 * ADVECTION) * (ring_n - ring_s))[0:1, :]
            brow[step, x + 1:x + 2, :] = ((0.25 * ADVECTION) * (ring_e - ring_w))[0:1, :]
            forward_row(step, x, row * tiles, corner, None, True, False)
            ring.append((
                h_ring, next_height(h_ring, ring_e, ring_w, ring_n, ring_s, row_of(wet, x + 1), row_of(mrow, x + 1)),
            ))
        h_w = jnp.where(first_row, ring[0][0], h_w)
        h_e = jnp.where(last_row, ring[1][0], h_e)
        brow[step, 1:SUB + 1, :] = (0.25 * ADVECTION) * (h_e - h_w)
        for x in (0, SUB - 1):
            forward_row(step, x, x * tiles, columns, None, True, True)
        h_next = next_height(h, h_e, h_w, h_n, h_s, wet_tile, mrow[1:SUB + 1, :])

        def strip_sides(value, from_e, from_w):
            e = jnp.where(lane >= span - width, roll_lanes(from_e, span - width), roll_lanes(value, LANE - width))
            w = jnp.where(lane < width, roll_lanes(from_w, LANE - span + width), roll_lanes(value, width))
            return e, w

        own = packs[step, 0]
        own_h = packs[step, 2]
        c_e, c_w = strip_sides(columns, corner_e, corner_w)
        c_n, c_s = jnp.where(even, far_columns, own), jnp.where(even, own, far_columns)
        s_e, s_w = strip_sides(strip_h, corner_he, corner_hw)
        s_n, s_s = jnp.where(even, far_h, own_h), jnp.where(even, own_h, far_h)
        down, up = roll_rows(columns, 1), roll_rows(columns, SUB - 1)
        upper = jnp.where(first_row, jnp.where(top_tile, columns, roll_lanes(down, 2)), down)
        lower = jnp.where(last_row, jnp.where(low_tile, columns, roll_lanes(up, LANE - 2)), up)
        a = (-0.25 * ADVECTION) * (s_n - s_s)
        b = (0.25 * ADVECTION) * (s_e - s_w)
        lap = c_e + c_w + c_n + c_s - 4.0 * columns
        strip = columns + strip_wet * (
            strip_diff * lap - a * (c_e - c_w) - b * (c_n - c_s) + VERTICAL_MIX * (upper + lower - 2.0 * columns)
        )
        sums = jnp.broadcast_to(jnp.sum(columns, axis=0, keepdims=True), (SUB, LANE))
        total = sums
        for i in range(1, per):
            total = total + roll_lanes(sums, LANE - 2 * i)
        total = repeated(jnp.where(lead, total, 0.0))
        strip_h = next_height(strip_h, s_e, s_w, s_n, s_s, strip_wet, total)
        columns = jnp.where(inside, strip, 0.0)
        strip_h = jnp.where(inside, strip_h, 0.0)
        side = zero
        for x in range(SUB):
            side = jnp.where(sub == x, spread(strip_h, x * tiles), side)

        step += 1
        final = step == ITERS - 1
        h = h_next
        heights.append(h)
        h_n, h_s = along_latitude(h, side)
        h_w = jnp.where(first_row, ring[0][1], roll_rows(h, 1))
        h_e = jnp.where(last_row, ring[1][1], roll_rows(h, SUB - 1))
        arow[step, 1:SUB + 1, :] = (-0.25 * ADVECTION) * (h_n - h_s)
        brow[step, 1:SUB + 1, :] = (0.25 * ADVECTION) * (h_e - h_w)

        def second_body(x, packed, step=step, columns=columns, final=final):
            done = forward_row(step, x, x * tiles, columns, None if final else packed, not final, True)
            return packed if final else done

        if final:
            break
        packed = (zero, zero)
        for x in (0, 1, SUB - 2, SUB - 1):
            packed = second_body(x, packed)
        h_edges = next_height(h, h_e, h_w, h_n, h_s, wet_tile, mrow[1:SUB + 1, :])
        row_copies = send_rows(step + 1, h_edges)
        corner_copies = send_corners(step + 1, packed[0], h_edges)
        packed = rows_of(second_body, 2, SUB - 2, packed)
        h = next_height(h, h_e, h_w, h_n, h_s, wet_tile, mrow[1:SUB + 1, :])
        heights.append(h)
        column_copies = send_columns(step + 1, packed[0], packed[1], h)

    def add_rows(step):
        for t in range(tiles):
            rows = slice(t * SUB, (t + 1) * SUB)
            lam[0, rows, :] = lam[0, rows, :] + slab_r[step, 0, rows, :]
            lam[SUB - 1, rows, :] = lam[SUB - 1, rows, :] + slab_r[step, 1, rows, :]

    def height_arrivals(step, lam_h, columns):
        lam_h = lam_h + jnp.where(edge_lane, spread(columns, hslot), 0.0)
        lam_h = lam_h + jnp.where(first_row, jnp.broadcast_to(slab_r[step, 0, hrow:hrow + 1, :], (SUB, LANE)), 0.0)
        return lam_h + jnp.where(last_row, jnp.broadcast_to(slab_r[step, 1, hrow:hrow + 1, :], (SUB, LANE)), 0.0)

    lam_h = hw_ref[...]
    columns = None
    for step in reversed(range(ITERS)):
        if step < ITERS - 1:
            wait_all(column_copies)
            columns = unpacked(bpackr[step + 1, 0], bpackr[step + 1, 1])

        def gather_body(x, packed):
            b = row_of(brow.at[step], x + 1)
            w = row_of(wet, x + 1)
            gu = zero
            gv = zero
            for t in range(tiles):
                rows = slice(t * SUB, (t + 1) * SUB)
                value = lam[x, rows, :]
                if columns is not None:
                    value = value + jnp.where(edge_lane, spread(columns, x * tiles + t), 0.0)
                    lam[x, rows, :] = value
                m = w * value
                mu[x + 1, rows, :] = m
                bm = b * m
                dm = diff[t] * m
                packed = packed_with(packed, jnp.where(last_lane, dm - bm, dm + bm), x * tiles + t)
                gu = gu + m * (state[step, x + 3, rows, :] - state[step, x + 1, rows, :])
                gv = gv + m * dy[step, x, rows, :]
            gurow[pl.ds(x, 1), :] = jnp.sum(gu, axis=0, keepdims=True)
            gvrow[pl.ds(x, 1), :] = jnp.sum(gv, axis=0, keepdims=True)
            return packed

        def first_body(x, packed):
            second_body(x, 0)
            return gather_body(x, packed)

        def sides():
            gu = (-0.25 * ADVECTION) * gurow[...]
            gv = (-0.25 * ADVECTION) * gvrow[...]
            return spread_h + gv, spread_h - gv, spread_h - gu, spread_h + gu

        start = step == ITERS - 1
        if start:
            packed = first_body(SUB - 1, first_body(0, zero))
        else:
            packed = rows_of(gather_body, 1, SUB - 1, zero)
            wait_all(row_copies)
            add_rows(step + 1)
            lam_h = height_arrivals(step + 1, lam_h, columns)
            packed = gather_body(SUB - 1, gather_body(0, packed))
        spread_h = HEIGHT_DIFFUSION * lam_h
        to_e, to_w, to_n, to_s = sides()
        a_last = row_of(arow.at[step], SUB)
        a_first = row_of(arow.at[step], 1)
        for t in range(tiles):
            rows = slice(t * SUB, (t + 1) * SUB)
            slab_s[step, 0, rows, :] = (diff[t] - a_last) * mu[SUB, rows, :]
            slab_s[step, 1, rows, :] = (diff[t] + a_first) * mu[1, rows, :]
        slab_s[step, 0, hrow:hrow + SUB, :] = jnp.broadcast_to(to_e[SUB - 1:SUB, :], (SUB, LANE))
        slab_s[step, 1, hrow:hrow + SUB, :] = jnp.broadcast_to(to_w[0:1, :], (SUB, LANE))
        row_copies = exchange_rows(
            slab_s.at[step, 0], slab_r.at[step, 0], slab_s.at[step, 1], slab_r.at[step, 1], b_send, b_recv, step,
        )
        if start:
            packed = rows_of(first_body, 1, SUB - 1, packed)
            to_e, to_w, to_n, to_s = sides()
        bpacks[step] = packed_with(packed, jnp.where(last_lane, to_n, to_s), hslot)
        column_copies = exchange_columns(bpacks.at[step], bpackr, b_send, b_recv, step)

        mrow[0:SUB, :] = (BUOYANCY / levels) * wet_tile * lam_h

        def local_body(x, carry):
            a_w = row_of(arow.at[step], x)
            a_e = row_of(arow.at[step], x + 2)
            b = row_of(brow.at[step], x + 1)
            centre = [mu[x + 1, t * SUB:(t + 1) * SUB, :] for t in range(tiles)]
            vert = vertical(centre)
            push = row_of(mrow, x)
            for t in range(tiles):
                rows = slice(t * SUB, (t + 1) * SUB)
                m = centre[t]
                m_w = mu[x, rows, :]
                m_e = mu[x + 2, rows, :]
                bm = b * m
                dm = diff[t] * m
                from_s = jnp.where(first_lane, 0.0, roll_lanes(dm - bm, 1))
                from_n = jnp.where(last_lane, 0.0, roll_lanes(dm + bm, LANE - 1))
                value = lam[x, rows, :] + VERTICAL_MIX * vert[t] - 4.0 * dm + from_s + from_n
                value = value + diff[t] * (m_w + m_e) + (a_e * m_e - a_w * m_w)
                if t < per:
                    value = value + push
                lam[x, rows, :] = value
            return carry

        rows_of(local_body, 0, SUB, 0)
        damp = jnp.tanh(heights[step])
        lam_h = (
            lam_h - 4.0 * spread_h - HEIGHT_DAMPING * (1.0 - damp * damp) * lam_h
            + jnp.where(first_row, 0.0, roll_rows(to_e, 1)) + jnp.where(last_row, 0.0, roll_rows(to_w, SUB - 1))
            + jnp.where(first_lane, 0.0, roll_lanes(to_n, 1)) + jnp.where(last_lane, 0.0, roll_lanes(to_s, LANE - 1))
        )

    wait_all(column_copies)
    columns = unpacked(bpackr[0, 0], bpackr[0, 1])

    def write_row(x):
        for t in range(tiles):
            value = lam[x, t * SUB:(t + 1) * SUB, :] + jnp.where(edge_lane, spread(columns, x * tiles + t), 0.0)
            out_ref[pl.ds(t * SUB * SUB + x, SUB, stride=SUB), :] = value

    for x in range(1, SUB - 1):
        write_row(x)
    wait_all(row_copies)
    add_rows(0)
    write_row(0)
    write_row(SUB - 1)
    outh_ref[...] = height_arrivals(0, lam_h, columns)

    for copy in a2a + sends:
        copy.wait_send()


def local(checkpoint, holder_list, height, land_mask, diffusivity, tracer_weight, height_weight):
    n, n_y = lax.axis_size("gx"), lax.axis_size("gy")
    width_x, width_y = height.shape
    assert (width_x, width_y) == (SUB, LANE)
    levels = diffusivity.shape[1]
    channels = 3 * levels
    piece_rows = checkpoint.shape[3] // LANE
    padded = -(-piece_rows // SUB) * SUB
    rows = channels + SUB
    f32 = jnp.float32
    vmem = pl.BlockSpec(memory_space=pltpu.VMEM)
    tile = pltpu.VMEM((SUB, LANE), f32)
    out, out_h = pl.pallas_call(
        functools.partial(kernel, n, n_y, levels, piece_rows),
        out_shape=(
            jax.ShapeDtypeStruct((channels * SUB, LANE), f32),
            jax.ShapeDtypeStruct((SUB, LANE), f32),
        ),
        in_specs=[pl.BlockSpec(memory_space=pltpu.HBM)] * 7,
        out_specs=(vmem, vmem),
        scratch_shapes=[
            pltpu.VMEM((n * padded, LANE), f32),
            pltpu.VMEM((n, padded, LANE), f32),
            pltpu.VMEM((ITERS, SUB + 4, rows, LANE), f32),
            pltpu.VMEM((ITERS, SUB, channels, LANE), f32),
            pltpu.VMEM((channels * SUB, LANE), f32),
            pltpu.VMEM((SUB, channels, LANE), f32),
            pltpu.VMEM((SUB + 2, channels, LANE), f32),
            pltpu.VMEM((2 * SUB, LANE), f32),
            pltpu.VMEM((ITERS, 2 * SUB, LANE), f32),
            pltpu.VMEM((ITERS, 2 * SUB, LANE), f32),
            pltpu.VMEM((2 * SUB, LANE), f32),
            tile, tile,
            pltpu.VMEM((ITERS, 5, SUB, LANE), f32),
            pltpu.VMEM((ITERS, 2, 5, SUB, LANE), f32),
            pltpu.VMEM((ITERS, 2, SUB, LANE), f32),
            pltpu.VMEM((ITERS, 4, 2, SUB, LANE), f32),
            pltpu.VMEM((ITERS, 2, rows, LANE), f32),
            pltpu.VMEM((ITERS, 2, rows, LANE), f32),
            pltpu.VMEM((ITERS, SUB, LANE), f32),
            pltpu.VMEM((ITERS, 2, SUB, LANE), f32),
            pltpu.SMEM(holder_list.shape, jnp.int32),
            pltpu.SMEM(diffusivity.shape, f32),
            pltpu.VMEM(checkpoint.shape[2:], f32),
            tile,
            pltpu.VMEM((SUB, LANE), jnp.int32),
            tile,
            pltpu.SemaphoreType.DMA((n,)),
            pltpu.SemaphoreType.DMA((n,)),
            pltpu.SemaphoreType.DMA((ITERS, 8)),
            pltpu.SemaphoreType.DMA((ITERS, 8)),
            pltpu.SemaphoreType.DMA((ITERS, 4)),
            pltpu.SemaphoreType.DMA((ITERS, 4)),
            pltpu.SemaphoreType.DMA((7,)),
        ],
        compiler_params=pltpu.CompilerParams(
            collective_id=0, has_side_effects=True, vmem_limit_bytes=60 * 2**20
        ),
    )(
        holder_list, diffusivity, checkpoint.reshape(checkpoint.shape[2:]), height, land_mask,
        tracer_weight.reshape(channels * SUB, LANE), height_weight,
    )
    return out.reshape(tracer_weight.shape), out_h


def solution(mesh):
    return jax.shard_map(
        local,
        mesh=mesh,
        in_specs=(
            P(("member", "gx"), "gy", None, None),
            P(("member", "gx"), "gy", None),
            P(("member", "gx"), "gy"),
            P("gx", "gy"),
            P(),
            P("member", None, "gx", "gy"),
            P(("member", "gx"), "gy"),
        ),
        out_specs=(P("member", None, "gx", "gy"), P(("member", "gx"), "gy")),
        check_vma=False,
    )
```
